128 devices in a mesh: fly: 16 (over y, z), sub: 8 (over x, core).
Axes of the slice: x: 4, y: 4, z: 4, core: 2. Of those that a mesh axis runs over, the one named last changes fastest.
Arguments:
- matrix: float32 [16384, 2048], P(('fly', 'sub'))
- row_signs: int32 [16384], P(('fly', 'sub')), may hold values from -1 to 1, as said below
- sample_idx: int32 [4096], P(('fly', 'sub')), may hold values from 0 to 127, as said below
- ridge_shift: float32 [1], replicated, may hold values from 0.5 to 1.5
Outputs:
- chol: float32 [2048, 2048], P(('fly', 'sub'))
- col_norms: float32 [2048], replicated
The draws below stay inside these ranges and needn't reach their ends.
Inputs may be any that keep to these rules, and one draw needn't show every extreme that they name: `sample_idx`: within each aligned block of 32 entries the row numbers are distinct. `row_signs`: each entry is -1 or 1.
All inputs are finite; a program needn't handle non-finite values.
Results may differ from the reference program's by a relative error of at most 0.00022.
Values sent between devices are 32-bit elements; how exact they have to be, the bound alone decides.
No kernel may reach another device: no remote copies, remote signals or barrier semaphores. Data moves between devices by JAX's collectives and lax.ppermute only.
A program may use at most 192 MiB of HBM per device.

```python
import math
import jax
import jax.numpy as jnp
from jax import lax

N = 2048
ROWS_DEV = 128
SAMP_DEV = 32
ROWS = 16384
SAMPLES = 4096


def draw_matrix(key, part):
    key = jax.random.fold_in(key, 3)
    keys = jax.random.split(key, 3)
    row_exp = jax.random.uniform(keys[1], (ROWS, 1), jnp.float32, 0.0, 1.0)
    trend = 1.0 + 2.0 * jnp.arange(ROWS, dtype=jnp.float32)[:, None] / ROWS
    row_scale = jnp.power(10.0, row_exp) * trend
    col_exp = jax.random.uniform(keys[2], (1, N), jnp.float32, -0.5, 0.5)
    col_scale = jnp.power(10.0, col_exp)
    entries = jax.random.normal(keys[0], (ROWS, N), jnp.float32)
    return (entries * row_scale * col_scale).astype(jnp.float32)


def draw_row_signs(key, part):
    key = jax.random.fold_in(key, 7)
    return (2 * jax.random.randint(key, (ROWS,), 0, 2) - 1).astype(jnp.int32)


def draw_sample_idx(key, part):
    key = jax.random.fold_in(key, 11)
    blocks = SAMPLES // SAMP_DEV
    keys = jax.random.split(key, blocks)
    perms = jax.vmap(lambda single: jax.random.permutation(single, ROWS_DEV))(keys)[:, :SAMP_DEV]
    target = jnp.where(jnp.arange(blocks) % 2 == 0, ROWS_DEV - 1, 0)[:, None]
    chosen = (perms + target - perms[:, :1]) % ROWS_DEV
    return chosen.reshape(-1).astype(jnp.int32)


def setup_inputs(seed: int = 0) -> dict:
    splits = jax.random.split(jax.random.key(seed), 5)
    matrix = draw_matrix(jax.random.fold_in(splits[4], 71), 0)
    row_signs = draw_row_signs(jax.random.fold_in(splits[4], 71), 0)
    sample_idx = draw_sample_idx(jax.random.fold_in(splits[4], 71), 0)
    ridge_shift = jnp.clip(jax.random.uniform(splits[3], (1,), jnp.float32, 0.5, 1.5), 0.5, 1.5)
    return dict(matrix=matrix, row_signs=row_signs, sample_idx=sample_idx, ridge_shift=ridge_shift)


def walsh_rows(values):
    total_rows = values.shape[0]
    columns = values.shape[1]
    half_span = 1
    while half_span < total_rows:
        shaped = values.reshape(total_rows // (2 * half_span), 2, half_span, columns)
        upper = shaped[:, 0]
        lower = shaped[:, 1]
        values = jnp.stack([upper + lower, upper - lower], axis=1).reshape(total_rows, columns)
        half_span = half_span * 2
    return values

def reference(matrix, row_signs, sample_idx, ridge_shift):
    col_squares = lax.optimization_barrier(jnp.sum(matrix * matrix, axis=0))
    col_norms = jnp.sqrt(col_squares / ROWS + 1e-06)
    signed = matrix * row_signs.astype(jnp.float32)[:, None] / col_norms[None, :]
    sketched = walsh_rows(signed) / math.sqrt(ROWS)
    offsets = jnp.arange(SAMPLES, dtype=jnp.int32) // SAMP_DEV * ROWS_DEV
    picked = jnp.take(sketched, (sample_idx + offsets).astype(jnp.int32), axis=0)
    gram_full = jnp.dot(picked.T.astype(jnp.float32), picked.astype(jnp.float32), precision=lax.Precision.HIGHEST, preferred_element_type=jnp.float32) / SAMPLES
    gram_full = gram_full + ridge_shift[0] * jnp.eye(N, dtype=jnp.float32)
    chol = jnp.linalg.cholesky(gram_full)
    return (chol, col_norms)
```

```python
import functools
import math

import jax
import jax.numpy as jnp
import numpy as np
from jax import lax
from jax.experimental import pallas as pl
from jax.experimental.pallas import tpu as pltpu
from jax.sharding import PartitionSpec as P

F32 = jnp.float32
BF16 = jnp.bfloat16
BLK = 128
VREG = (8, 128)
AXES = ("fly", "sub")


def sylvester(order):
    idx = np.arange(order)
    common = idx[:, None] & idx[None, :]
    parity = np.zeros((order, order), np.int64)
    for bit in range(order.bit_length() - 1):
        parity ^= common >> bit & 1
    return (1 - 2 * parity).astype(np.float32)


def halves(value):
    high = value.astype(BF16)
    return high, (value - high.astype(F32)).astype(BF16)


def thirds(value):
    high = value.astype(BF16)
    rest = value - high.astype(F32)
    mid = rest.astype(BF16)
    return high, mid, (rest - mid.astype(F32)).astype(BF16)


def contract(a, b, dims):
    return lax.dot_general(a, b, (dims, ((), ())), preferred_element_type=F32)


def contract_split(a, b, dims):
    return contract(a[0], b[0], dims) + (contract(a[0], b[1], dims) + contract(a[1], b[0], dims))


NT = ((1,), (1,))
TN = ((0,), (0,))
NN = ((1,), (0,))


def factor(d_ref, u_ref, inv_ref, cols_ref, rows_ref, irows_ref):
    groups = BLK // 8
    sublane = lax.broadcasted_iota(jnp.int32, VREG, 0)
    lane = lax.broadcasted_iota(jnp.int32, VREG, 1)
    block = [d_ref[8 * g : 8 * g + 8, :] for g in range(groups)]
    inverse = [jnp.where(lane == sublane + 8 * g, 1.0, 0.0).astype(F32) for g in range(groups)]
    for t in range(groups):
        cols = {
            g: [jnp.broadcast_to(block[g][:, 8 * t + c : 8 * t + c + 1], VREG) for c in range(8)]
            for g in range(t, groups)
        }
        cbase, rbase = 64 * (t % 2), 8 * (t % 2)
        for c in range(8):
            cols_ref[cbase + 8 * c : cbase + 8 * c + 8, :] = cols[t][c]
        rows_ref[rbase : rbase + 8, :] = block[t]
        irows_ref[rbase : rbase + 8, :] = inverse[t]
        d = {}
        for k in range(8):
            for i in range(k + 1):
                at = cbase + 8 * k + i
                d[i, k] = jnp.broadcast_to(cols_ref[at : at + 1, :], VREG)
        r = [jnp.broadcast_to(rows_ref[rbase + i : rbase + i + 1, :], VREG) for i in range(8)]
        w = [jnp.broadcast_to(irows_ref[rbase + i : rbase + i + 1, :], VREG) for i in range(8)]
        s, inv, u, v = {}, [None] * 8, [None] * 8, [None] * 8
        for i in range(0, 8, 2):
            a, b, c = d[i, i], d[i, i + 1], d[i + 1, i + 1]
            det = a * c - b * b
            rdet = 1.0 / det
            ra = lax.rsqrt(a)
            l10 = b * ra
            rc = lax.rsqrt(det) * (a * ra)
            inv[i], inv[i + 1] = ra, rc
            s[i, i + 1] = l10
            u[i], v[i] = r[i] * ra, w[i] * ra
            u[i + 1] = (r[i + 1] - l10 * u[i]) * rc
            v[i + 1] = (w[i + 1] - l10 * v[i]) * rc
            later = range(i + 2, 8)
            for k in later:
                s[i, k] = d[i, k] * ra
                s[i + 1, k] = (d[i + 1, k] - l10 * s[i, k]) * rc
            x = {k: c * d[i, k] - b * d[i + 1, k] for k in later}
            y = {k: a * d[i + 1, k] - b * d[i, k] for k in later}
            for k in later:
                for m in range(k, 8):
                    d[k, m] = d[k, m] - (x[k] * d[i, m] + y[k] * d[i + 1, m]) * rdet
                r[k] = r[k] - (s[i, k] * u[i] + s[i + 1, k] * u[i + 1])
                w[k] = w[k] - (s[i, k] * v[i] + s[i + 1, k] * v[i + 1])
        for i in range(8):
            at = 8 * t + i
            u_ref[at : at + 1, :] = u[i][0:1, :]
            inv_ref[at : at + 1, :] = v[i][0:1, :]
        if t == groups - 1:
            break
        q, z = list(u), list(v)
        for i in range(7, -1, -1):
            for k in range(i + 1, 8):
                q[i] = q[i] - s[i, k] * q[k]
                z[i] = z[i] - s[i, k] * z[k]
            q[i], z[i] = q[i] * inv[i], z[i] * inv[i]

        def total(column, row):
            t0 = [column[c] * row[c] for c in range(8)]
            return ((t0[0] + t0[1]) + (t0[2] + t0[3])) + ((t0[4] + t0[5]) + (t0[6] + t0[7]))

        for g in range(t + 1, groups):
            block[g] = block[g] - total(cols[g], q)
            inverse[g] = inverse[g] - total(cols[g], z)


CHUNK = 256


def chol_kernel(
    fly,
    sub,
    place_ref,
    ridge_ref,
    gram_ref,
    out_ref,
    a_ref,
    high_ref,
    rest_ref,
    s_ref,
    d_ref,
    u_ref,
    inv_ref,
    cols_ref,
    rows_ref,
    irows_ref,
    sems,
):
    share, columns = out_ref.shape
    blocks = columns // BLK
    piece = a_ref.shape[0] // (fly * sub)
    stride = piece * fly

    def start(i, _):
        s, f = i // fly, i % fly
        pltpu.make_async_copy(
            gram_ref.at[f * sub + s, pl.ds(0, piece)],
            a_ref.at[pl.ds(pl.multiple_of(i * piece, 8), piece)],
            sems.at[s],
        ).start()
        return 0

    lax.fori_loop(0, fly * sub, start, 0)
    high_ref[...] = jnp.zeros_like(high_ref)
    rest_ref[...] = jnp.zeros_like(rest_ref)
    place = place_ref[0]
    mine = place * share
    mine_block = mine // BLK
    sub_i = lax.broadcasted_iota(jnp.int32, (BLK, BLK), 0)
    lane_i = lax.broadcasted_iota(jnp.int32, (BLK, BLK), 1)
    eye = jnp.where(sub_i == lane_i, ridge_ref[0], 0.0)

    def panel(k, _):
        @pl.when(k < sub)
        def _():
            at = pl.ds(pl.multiple_of(k * stride, 8), stride)
            pltpu.make_async_copy(a_ref.at[at], a_ref.at[at], sems.at[k]).wait()

        other = blocks - 1 - k
        off = jnp.where(k < sub, k * stride, other * stride + (blocks - other) * BLK)
        top = k * BLK
        lanes = pl.ds(pl.multiple_of(top, BLK), BLK)
        mine_rows = pl.ds(pl.multiple_of(top, BLK), BLK)
        depth = pl.cdiv(k * BLK, CHUNK)

        def rows_of(i):
            return pl.ds(pl.multiple_of(top + i * BLK, BLK), BLK)

        def gather(i, _):
            a = a_ref[pl.ds(pl.multiple_of(off + i * BLK, 8), BLK), :]
            at = rows_of(i)

            def step(c, acc):
                cols = pl.ds(pl.multiple_of(c * CHUNK, CHUNK), CHUNK)
                here = high_ref[at, cols], rest_ref[at, cols]
                there = high_ref[mine_rows, cols], rest_ref[mine_rows, cols]
                return acc - contract_split(here, there, NT)

            s_ref[at, :] = lax.fori_loop(0, depth, step, a)
            return 0

        lax.fori_loop(0, blocks - k, gather, 0)
        d_ref[...] = s_ref[mine_rows, :] + eye
        factor(d_ref, u_ref, inv_ref, cols_ref, rows_ref, irows_ref)
        inverse = halves(inv_ref[...])
        s_ref[mine_rows, :] = jnp.where(sub_i >= lane_i, u_ref[...].T, 0.0)

        def solve(i, _):
            at = rows_of(i)
            low = contract_split(halves(s_ref[at, :]), inverse, NT)
            s_ref[at, :] = low
            high, rest = halves(low)
            high_ref[at, lanes] = high
            rest_ref[at, lanes] = rest
            return 0

        lax.fori_loop(1, blocks - k, solve, 0)
        own = s_ref[pl.ds(pl.multiple_of(mine, share), share), :]
        out_ref[:, lanes] = jnp.where(mine_block >= k, own, 0.0)
        return 0

    lax.fori_loop(0, blocks, panel, 0)


def factored(place, ridge, full, fly, sub, share):
    columns = share * fly * sub
    piece = (columns + BLK) // fly
    smem = pl.BlockSpec(memory_space=pltpu.SMEM)
    return pl.pallas_call(
        functools.partial(chol_kernel, fly, sub),
        out_shape=jax.ShapeDtypeStruct((share, columns), F32),
        in_specs=[smem, smem, pl.BlockSpec(memory_space=pl.ANY)],
        scratch_shapes=[
            pltpu.VMEM((piece * fly * sub, BLK), F32),
            pltpu.VMEM((columns, columns), BF16),
            pltpu.VMEM((columns, columns), BF16),
            pltpu.VMEM((columns, BLK), F32),
            pltpu.VMEM((BLK, BLK), F32),
            pltpu.VMEM((BLK, BLK), F32),
            pltpu.VMEM((BLK, BLK), F32),
            pltpu.VMEM((BLK, BLK), F32),
            pltpu.VMEM((16, BLK), F32),
            pltpu.VMEM((16, BLK), F32),
            pltpu.SemaphoreType.DMA((sub,)),
        ],
        compiler_params=pltpu.CompilerParams(vmem_limit_bytes=52 << 20),
        name="cholesky",
    )(place, ridge, full)


def across_kernel(x_ref, table_ref, y_ref, norm_ref):
    devices = table_ref.shape[0]
    per = x_ref.shape[0] // devices
    lanes = lax.broadcasted_iota(jnp.int32, VREG, 1)
    norms = jnp.zeros(VREG, F32)
    total = devices * x_ref.shape[1]
    table = table_ref[...]
    for col in range(per):
        rows = x_ref[pl.ds(col, devices, stride=per), :]
        squares = jnp.sum(jnp.sum(rows * rows, axis=0, keepdims=True), axis=1, keepdims=True)
        norm = jnp.sqrt(jnp.broadcast_to(squares, VREG) / total + 1e-06)
        norms = jnp.where(lanes == col, norm, norms)
        scale = 1.0 / (norm[0:1, :] * math.sqrt(total))
        high, mid, low = thirds(rows)
        mixed = contract(table, high, NN) + (contract(table, mid, NN) + contract(table, low, NN))
        y_ref[pl.ds(col, devices, stride=per), :] = mixed * scale
    norm_ref[...] = norms


def across(x, table):
    return pl.pallas_call(
        across_kernel,
        out_shape=[jax.ShapeDtypeStruct(x.shape, F32), jax.ShapeDtypeStruct(VREG, F32)],
        compiler_params=pltpu.CompilerParams(vmem_limit_bytes=32 << 20),
        name="across_devices",
    )(x, table)


def gram_kernel(sub_ref, *refs):
    picks, out_ref, high_ref, rest_ref = refs[:-3], refs[-3], refs[-2], refs[-1]
    sub = sub_ref[0]
    samples, columns = picks[0].shape
    blocks = columns // BLK
    for i, ref in enumerate(picks):
        high, rest = halves(ref[...])
        high_ref[i * samples : (i + 1) * samples, :] = high
        rest_ref[i * samples : (i + 1) * samples, :] = rest

    def block(index):
        at = pl.ds(pl.multiple_of(index * BLK, BLK), BLK)
        return high_ref[:, at], rest_ref[:, at]

    for j in range(blocks + 1):
        first = j < blocks - sub
        row = jnp.where(first, sub + j, j - 1)
        col = jnp.where(first, sub, blocks - 1 - sub)
        out_ref[j * BLK : (j + 1) * BLK, :] = contract_split(block(row), block(col), TN)


def gram_share(sub, picks):
    samples, columns = picks[0].shape
    rows = samples * len(picks)
    return pl.pallas_call(
        gram_kernel,
        out_shape=jax.ShapeDtypeStruct((columns + BLK, BLK), F32),
        in_specs=[pl.BlockSpec(memory_space=pltpu.SMEM)]
        + [pl.BlockSpec(memory_space=pltpu.VMEM)] * len(picks),
        scratch_shapes=[pltpu.VMEM((rows, columns), BF16)] * 2,
        compiler_params=pltpu.CompilerParams(vmem_limit_bytes=32 << 20),
        name="gram_share",
    )(sub, *picks)


def shards(matrix, row_signs, sample_idx, ridge_shift):
    rows_here, columns = matrix.shape
    fly, sub = lax.axis_size("fly"), lax.axis_size("sub")
    devices = fly * sub
    place = lax.axis_index(AXES)
    samples_all = sample_idx.shape[0] * devices
    per = columns // devices
    signed = (matrix * row_signs.astype(F32)[:, None]).T
    spread = lax.all_to_all(signed.reshape(devices, per, rows_here), AXES, 0, 0, tiled=True)
    table = jnp.asarray(sylvester(devices), BF16)
    mixed, norms = across(spread.reshape(columns, rows_here), table)
    back = lax.all_to_all(mixed.reshape(devices, per, rows_here), AXES, 0, 0, tiled=True)
    chosen = jnp.take(jnp.asarray(sylvester(rows_here)), sample_idx, axis=0)
    picked = lax.dot_general(
        chosen,
        back.reshape(columns, rows_here),
        (NT, ((), ())),
        precision=lax.Precision.HIGHEST,
        preferred_element_type=F32,
    )
    picks = [picked]
    for step in range(1, sub):
        picks.append(lax.ppermute(picked, "sub", [(i, (i + step) % sub) for i in range(sub)]))
    share = gram_share(lax.axis_index("sub").astype(jnp.int32)[None], picks)
    piece = (columns + BLK) // fly
    parts = lax.all_to_all(share.reshape(fly, piece, BLK), "fly", 0, 0, tiled=True)
    summed = jnp.sum(parts, axis=0) / samples_all
    full = lax.all_gather(jnp.concatenate([summed, norms], axis=0), AXES)
    chol = factored(place.astype(jnp.int32)[None], ridge_shift, full, fly, sub, per)
    col_norms = full[:, piece, :per].reshape(columns)
    return (chol, col_norms)


def solution(mesh):
    in_specs = (P(AXES, None), P(AXES), P(AXES), P())
    out_specs = (P(AXES, None), P())
    return jax.shard_map(shards, mesh=mesh, in_specs=in_specs, out_specs=out_specs, check_vma=False)
```

```python
import functools
import math

import jax
import jax.numpy as jnp
import numpy as np
from jax import lax
from jax.experimental import pallas as pl
from jax.experimental.pallas import tpu as pltpu
from jax.sharding import PartitionSpec as P

F32 = jnp.float32
BF16 = jnp.bfloat16
BLK = 128
VREG = (8, 128)
AXES = ("fly", "sub")


def sylvester(order):
    idx = np.arange(order)
    common = idx[:, None] & idx[None, :]
    parity = np.zeros((order, order), np.int64)
    for bit in range(order.bit_length() - 1):
        parity ^= common >> bit & 1
    return (1 - 2 * parity).astype(np.float32)


def halves(value):
    high = value.astype(BF16)
    return high, (value - high.astype(F32)).astype(BF16)


def thirds(value):
    high = value.astype(BF16)
    rest = value - high.astype(F32)
    mid = rest.astype(BF16)
    return high, mid, (rest - mid.astype(F32)).astype(BF16)


def contract(a, b, dims):
    return lax.dot_general(a, b, (dims, ((), ())), preferred_element_type=F32)


def contract_split(a, b, dims):
    return contract(a[0], b[0], dims) + (contract(a[0], b[1], dims) + contract(a[1], b[0], dims))


NT = ((1,), (1,))
TN = ((0,), (0,))
NN = ((1,), (0,))
WIDE = 16


def factor(d_ref, u_ref, inv_ref):
    steps, tall = BLK // WIDE, WIDE // 8
    sublane = lax.broadcasted_iota(jnp.int32, VREG, 0)
    lane = lax.broadcasted_iota(jnp.int32, VREG, 1)
    groups = BLK // 8
    block = [d_ref[8 * g : 8 * g + 8, :] for g in range(groups)]
    inverse = [jnp.where(lane == sublane + 8 * g, 1.0, 0.0).astype(F32) for g in range(groups)]

    def row(parts, i):
        part = parts[i // 8]
        return jnp.broadcast_to(part[i % 8 : i % 8 + 1, :], VREG)

    def total(terms):
        while len(terms) > 1:
            terms = [terms[i] + terms[i + 1] for i in range(0, len(terms), 2)]
        return terms[0]

    for t in range(steps):
        first = t * tall

        def column(g, c):
            at = WIDE * t + c
            return jnp.broadcast_to(block[g][:, at : at + 1], VREG)

        mine = range(first, first + tall)
        cols = [[column(g, c) for g in mine] for c in range(WIDE)]
        raw = [block[g] for g in mine]
        r, w = list(raw), [inverse[g] for g in mine]
        after = range(first + tall, min(first + 2 * tall, groups))
        ahead = {g: [column(g, c) for c in range(WIDE)] for g in after}
        for i in range(0, WIDE, 2):
            v, lo = i // 8, i % 8
            is_i, is_j = sublane == lo, sublane == lo + 1
            pair = jnp.logical_or(is_i, is_j)
            a, b, c = row(cols[i], i), row(cols[i + 1], i), row(cols[i + 1], i + 1)
            det = a * c - b * b
            rdet = 1.0 / det
            ra = lax.rsqrt(a)
            l10 = b * ra
            rc = lax.rsqrt(det) * (a * ra)
            x = [c * p - b * q for p, q in zip(cols[i], cols[i + 1])]
            y = [a * q - b * p for p, q in zip(cols[i], cols[i + 1])]
            x[v] = jnp.where(is_i, -c, jnp.where(is_j, b, x[v]))
            y[v] = jnp.where(is_i, b, jnp.where(is_j, -a, y[v]))

            def sweep(parts):
                ri, rj = row(parts, i), row(parts, i + 1)
                out = []
                for n, part in enumerate(parts):
                    z = (x[n] * ri + y[n] * rj) * rdet
                    out.append((jnp.where(pair, 0.0, part) if n == v else part) - z)
                return out

            for m in range(i + 2, WIDE):
                cols[m] = sweep(cols[m])
            at = WIDE * t + i
            for parts, ref in ((r, u_ref), (w, inv_ref)):
                ui = row(parts, i) * ra
                uj = (row(parts, i + 1) - l10 * ui) * rc
                ref[at : at + 1, :] = ui[0:1]
                ref[at + 1 : at + 2, :] = uj[0:1]
            r, w = sweep(r), sweep(w)
        if t == steps - 1:
            break
        q = [row(r, c) for c in range(WIDE)]
        z = [row(w, c) for c in range(WIDE)]
        for g in after:
            block[g] = block[g] - total([ahead[g][c] * q[c] for c in range(WIDE)])
            inverse[g] = inverse[g] - total([ahead[g][c] * z[c] for c in range(WIDE)])
        if t + 2 < steps:
            xh, xm, xl = [p.astype(F32) for p in thirds(jnp.concatenate(raw, axis=0))]
            solved = jnp.concatenate([jnp.concatenate(r, axis=0), jnp.concatenate(w, axis=0)], axis=1)
            yh, ym, yl = [p.astype(F32) for p in thirds(solved)]
            left = jnp.concatenate([xh, xm, xh, xm, xl, xh], axis=0).astype(BF16)
            right = jnp.concatenate([yh, yh, ym, ym, yh, yl], axis=0).astype(BF16)
            update = contract(left, right, TN)
            for g in range(first + 2 * tall, groups):
                block[g] = block[g] - update[8 * g : 8 * g + 8, :BLK]
                inverse[g] = inverse[g] - update[8 * g : 8 * g + 8, BLK:]


SPAN = 4


def chol_kernel(
    fly,
    sub,
    place_ref,
    ridge_ref,
    gram_ref,
    out_ref,
    a_ref,
    high_ref,
    rest_ref,
    s_ref,
    d_ref,
    u_ref,
    inv_ref,
    sems,
):
    share, columns = out_ref.shape
    blocks = columns // BLK
    piece = a_ref.shape[0] // (fly * sub)
    stride = piece * fly
    wide = SPAN * BLK
    spans = blocks // SPAN

    def start(i, _):
        s, f = i // fly, i % fly
        pltpu.make_async_copy(
            gram_ref.at[f * sub + s, pl.ds(0, piece)],
            a_ref.at[pl.ds(pl.multiple_of(i * piece, 8), piece)],
            sems.at[s],
        ).start()
        return 0

    lax.fori_loop(0, fly * sub, start, 0)
    arrived = set()
    sub_i = lax.broadcasted_iota(jnp.int32, (BLK, BLK), 0)
    lane_i = lax.broadcasted_iota(jnp.int32, (BLK, BLK), 1)
    eye = jnp.where(sub_i == lane_i, ridge_ref[0], 0.0)

    def offset(k):
        other = blocks - 1 - k
        return k * stride if k < sub else other * stride + (blocks - other) * BLK

    for q in range(spans):
        left = q * wide
        for j in range(SPAN):
            k = q * SPAN + j
            owner = min(k, blocks - 1 - k)
            if owner not in arrived:
                arrived.add(owner)
                at = pl.ds(owner * stride, stride)
                pltpu.make_async_copy(a_ref.at[at], a_ref.at[at], sems.at[owner]).wait()
        for top in range(left, columns, wide):
            rows = slice(top, top + wide)
            if q:
                here = high_ref[rows, :left], rest_ref[rows, :left]
                there = high_ref[left : left + wide, :left], rest_ref[left : left + wide, :left]
                known = contract_split(here, there, NT)
            for j in range(SPAN):
                k = q * SPAN + j
                skip = j * BLK if top == left else 0
                lanes = slice(j * BLK, (j + 1) * BLK)
                at = offset(k) + top + skip - k * BLK
                value = a_ref[at : at + wide - skip, :]
                if q:
                    value = value - known[skip:, lanes]
                s_ref[top + skip : top + wide, lanes] = value

        def panel(j, _):
            top = pl.multiple_of(left + j * BLK, BLK)
            mine = pl.ds(top, BLK)
            here = pl.ds(pl.multiple_of(j * BLK, BLK), BLK)
            there = pl.ds(top, BLK)
            for depth in range(1, SPAN):

                @pl.when(j == depth)
                def _():
                    lanes = slice(depth * BLK, (depth + 1) * BLK)
                    cols = slice(left, left + depth * BLK)
                    at = left + depth * BLK
                    own = high_ref[at : at + BLK, cols], rest_ref[at : at + BLK, cols]
                    for first in range(left, columns, wide):
                        rows = slice(max(first, at), first + wide)
                        part = high_ref[rows, cols], rest_ref[rows, cols]
                        s_ref[rows, lanes] = s_ref[rows, lanes] - contract_split(part, own, NT)

            d_ref[...] = s_ref[mine, here] + eye
            factor(d_ref, u_ref, inv_ref)
            inverse = halves(inv_ref[...])
            for first in range(left, columns, wide):
                rows = slice(first, first + wide)
                high, rest = halves(contract_split(halves(s_ref[rows, here]), inverse, NT))
                high_ref[rows, there] = high
                rest_ref[rows, there] = rest
            high, rest = halves(u_ref[...].T)
            high_ref[mine, there] = high
            rest_ref[mine, there] = rest
            return 0

        lax.fori_loop(0, SPAN, panel, 0)
    mine = place_ref[0] * share
    at = pl.ds(pl.multiple_of(mine, share), share)
    row = lax.broadcasted_iota(jnp.int32, (share, columns), 0) + mine
    col = lax.broadcasted_iota(jnp.int32, (share, columns), 1)
    value = high_ref[at, :].astype(F32) + rest_ref[at, :].astype(F32)
    out_ref[...] = jnp.where(col <= row, value, 0.0)


def factored(place, ridge, full, fly, sub, share):
    columns = share * fly * sub
    piece = (columns + BLK) // fly
    smem = pl.BlockSpec(memory_space=pltpu.SMEM)
    return pl.pallas_call(
        functools.partial(chol_kernel, fly, sub),
        out_shape=jax.ShapeDtypeStruct((share, columns), F32),
        in_specs=[smem, smem, pl.BlockSpec(memory_space=pl.ANY)],
        scratch_shapes=[
            pltpu.VMEM((piece * fly * sub, BLK), F32),
            pltpu.VMEM((columns, columns), BF16),
            pltpu.VMEM((columns, columns), BF16),
            pltpu.VMEM((columns, SPAN * BLK), F32),
            pltpu.VMEM((BLK, BLK), F32),
            pltpu.VMEM((BLK, BLK), F32),
            pltpu.VMEM((BLK, BLK), F32),
            pltpu.SemaphoreType.DMA((sub,)),
        ],
        compiler_params=pltpu.CompilerParams(vmem_limit_bytes=52 << 20),
        name="cholesky",
    )(place, ridge, full)


def across_kernel(x_ref, table_ref, y_ref, norm_ref):
    devices = table_ref.shape[0]
    per = x_ref.shape[0] // devices
    lanes = lax.broadcasted_iota(jnp.int32, VREG, 1)
    norms = jnp.zeros(VREG, F32)
    total = devices * x_ref.shape[1]
    table = table_ref[...]
    for col in range(per):
        rows = x_ref[pl.ds(col, devices, stride=per), :]
        squares = jnp.sum(jnp.sum(rows * rows, axis=0, keepdims=True), axis=1, keepdims=True)
        norm = jnp.sqrt(jnp.broadcast_to(squares, VREG) / total + 1e-06)
        norms = jnp.where(lanes == col, norm, norms)
        scale = 1.0 / (norm[0:1, :] * math.sqrt(total))
        high, mid, low = thirds(rows)
        mixed = contract(table, high, NN) + (contract(table, mid, NN) + contract(table, low, NN))
        y_ref[pl.ds(col, devices, stride=per), :] = mixed * scale
    norm_ref[...] = norms


def across(x, table):
    return pl.pallas_call(
        across_kernel,
        out_shape=[jax.ShapeDtypeStruct(x.shape, F32), jax.ShapeDtypeStruct(VREG, F32)],
        compiler_params=pltpu.CompilerParams(vmem_limit_bytes=32 << 20),
        name="across_devices",
    )(x, table)


def gram_kernel(sub_ref, *refs):
    picks, out_ref, high_ref, rest_ref = refs[:-3], refs[-3], refs[-2], refs[-1]
    sub = sub_ref[0]
    samples, columns = picks[0].shape
    blocks = columns // BLK
    for i, ref in enumerate(picks):
        high, rest = halves(ref[...])
        high_ref[i * samples : (i + 1) * samples, :] = high
        rest_ref[i * samples : (i + 1) * samples, :] = rest

    def block(index):
        at = pl.ds(pl.multiple_of(index * BLK, BLK), BLK)
        return high_ref[:, at], rest_ref[:, at]

    for j in range(blocks + 1):
        first = j < blocks - sub
        row = jnp.where(first, sub + j, j - 1)
        col = jnp.where(first, sub, blocks - 1 - sub)
        out_ref[j * BLK : (j + 1) * BLK, :] = contract_split(block(row), block(col), TN)


def gram_share(sub, picks):
    samples, columns = picks[0].shape
    rows = samples * len(picks)
    return pl.pallas_call(
        gram_kernel,
        out_shape=jax.ShapeDtypeStruct((columns + BLK, BLK), F32),
        in_specs=[pl.BlockSpec(memory_space=pltpu.SMEM)]
        + [pl.BlockSpec(memory_space=pltpu.VMEM)] * len(picks),
        scratch_shapes=[pltpu.VMEM((rows, columns), BF16)] * 2,
        compiler_params=pltpu.CompilerParams(vmem_limit_bytes=32 << 20),
        name="gram_share",
    )(sub, *picks)


def shards(matrix, row_signs, sample_idx, ridge_shift):
    rows_here, columns = matrix.shape
    fly, sub = lax.axis_size("fly"), lax.axis_size("sub")
    devices = fly * sub
    place = lax.axis_index(AXES)
    samples_all = sample_idx.shape[0] * devices
    per = columns // devices
    signed = (matrix * row_signs.astype(F32)[:, None]).T
    spread = lax.all_to_all(signed.reshape(devices, per, rows_here), AXES, 0, 0, tiled=True)
    table = jnp.asarray(sylvester(devices), BF16)
    mixed, norms = across(spread.reshape(columns, rows_here), table)
    back = lax.all_to_all(mixed.reshape(devices, per, rows_here), AXES, 0, 0, tiled=True)
    chosen = jnp.take(jnp.asarray(sylvester(rows_here)), sample_idx, axis=0)
    picked = lax.dot_general(
        chosen,
        back.reshape(columns, rows_here),
        (NT, ((), ())),
        precision=lax.Precision.HIGHEST,
        preferred_element_type=F32,
    )
    picks = [picked]
    for step in range(2, sub, 2):
        picks.append(lax.ppermute(picked, "sub", [(i, (i + step) % sub) for i in range(sub)]))
    picks += [lax.ppermute(value, "sub", [(i, i ^ 1) for i in range(sub)]) for value in picks]
    share = gram_share(lax.axis_index("sub").astype(jnp.int32)[None], picks)
    piece = (columns + BLK) // fly
    parts = lax.all_to_all(share.reshape(fly, piece, BLK), "fly", 0, 0, tiled=True)
    summed = jnp.sum(parts, axis=0) / samples_all
    full = lax.all_gather(jnp.concatenate([summed, norms], axis=0), AXES)
    chol = factored(place.astype(jnp.int32)[None], ridge_shift, full, fly, sub, per)
    col_norms = full[:, piece, :per].reshape(columns)
    return (chol, col_norms)


def solution(mesh):
    in_specs = (P(AXES, None), P(AXES), P(AXES), P())
    out_specs = (P(AXES, None), P())
    return jax.shard_map(shards, mesh=mesh, in_specs=in_specs, out_specs=out_specs, check_vma=False)
```

```python
import functools
import math

import jax
import jax.numpy as jnp
import numpy as np
from jax import lax
from jax.experimental import pallas as pl
from jax.experimental.pallas import tpu as pltpu
from jax.sharding import PartitionSpec as P

F32 = jnp.float32
BF16 = jnp.bfloat16
BLK = 128
VREG = (8, 128)
AXES = ("fly", "sub")


def sylvester(order):
    idx = np.arange(order)
    common = idx[:, None] & idx[None, :]
    parity = np.zeros((order, order), np.int64)
    for bit in range(order.bit_length() - 1):
        parity ^= common >> bit & 1
    return (1 - 2 * parity).astype(np.float32)


def halves(value):
    high = value.astype(BF16)
    return high, (value - high.astype(F32)).astype(BF16)


def thirds(value):
    high = value.astype(BF16)
    rest = value - high.astype(F32)
    mid = rest.astype(BF16)
    return high, mid, (rest - mid.astype(F32)).astype(BF16)


def contract(a, b, dims):
    return lax.dot_general(a, b, (dims, ((), ())), preferred_element_type=F32)


def contract_split(a, b, dims):
    return contract(a[0], b[0], dims) + (contract(a[0], b[1], dims) + contract(a[1], b[0], dims))


NT = ((1,), (1,))
TN = ((0,), (0,))
NN = ((1,), (0,))
WIDE = 16


def factor(d_ref, u_ref, inv_ref, between=None):
    steps, tall = BLK // WIDE, WIDE // 8
    sublane = lax.broadcasted_iota(jnp.int32, VREG, 0)
    lane = lax.broadcasted_iota(jnp.int32, VREG, 1)
    groups = BLK // 8
    block = [d_ref[8 * g : 8 * g + 8, :] for g in range(groups)]
    inverse = [jnp.where(lane == sublane + 8 * g, 1.0, 0.0).astype(F32) for g in range(groups)]

    def row(parts, i):
        part = parts[i // 8]
        return jnp.broadcast_to(part[i % 8 : i % 8 + 1, :], VREG)

    def total(terms):
        while len(terms) > 1:
            terms = [terms[i] + terms[i + 1] for i in range(0, len(terms), 2)]
        return terms[0]

    for t in range(steps):
        first = t * tall

        def column(g, c):
            at = WIDE * t + c
            return jnp.broadcast_to(block[g][:, at : at + 1], VREG)

        mine = range(first, first + tall)
        cols = [[column(g, c) for g in mine] for c in range(WIDE)]
        raw = [block[g] for g in mine]
        r, w = list(raw), [inverse[g] for g in mine]
        after = range(first + tall, min(first + 2 * tall, groups))
        ahead = {g: [column(g, c) for c in range(WIDE)] for g in after}
        for i in range(0, WIDE, 2):
            v, lo = i // 8, i % 8
            is_i, is_j = sublane == lo, sublane == lo + 1
            a, b, c = row(cols[i], i), row(cols[i + 1], i), row(cols[i + 1], i + 1)
            det = a * c - b * b
            rdet = 1.0 / det
            ra = lax.rsqrt(a)
            l10 = b * ra
            rc = lax.rsqrt(det) * (a * ra)
            x = [c * p - b * q for p, q in zip(cols[i], cols[i + 1])]
            y = [a * q - b * p for p, q in zip(cols[i], cols[i + 1])]
            x[v] = jnp.where(is_i, det - c, jnp.where(is_j, b, x[v]))
            y[v] = jnp.where(is_i, b, jnp.where(is_j, det - a, y[v]))
            x, y = [p * rdet for p in x], [p * rdet for p in y]

            def sweep(parts):
                ri, rj = row(parts, i), row(parts, i + 1)
                return [part - x[n] * ri - y[n] * rj for n, part in enumerate(parts)]

            for m in range(i + 2, WIDE):
                cols[m] = sweep(cols[m])
            at = WIDE * t + i
            for parts, ref in ((r, u_ref), (w, inv_ref)):
                ui = row(parts, i) * ra
                uj = (row(parts, i + 1) - l10 * ui) * rc
                ref[at : at + 1, :] = ui[0:1]
                ref[at + 1 : at + 2, :] = uj[0:1]
            r, w = sweep(r), sweep(w)
        if between is not None:
            between(t)
        if t == steps - 1:
            break
        q = [row(r, c) for c in range(WIDE)]
        for g in after:
            block[g] = block[g] - total([ahead[g][c] * q[c] for c in range(WIDE)])
        if True:
            xh, xm, xl = [p.astype(F32) for p in thirds(jnp.concatenate(raw, axis=0))]
            solved = jnp.concatenate([jnp.concatenate(r, axis=0), jnp.concatenate(w, axis=0)], axis=1)
            yh, ym, yl = [p.astype(F32) for p in thirds(solved)]
            left = jnp.concatenate([xh, xm, xh, xm, xl, xh], axis=0).astype(BF16)
            right = jnp.concatenate([yh, yh, ym, ym, yh, yl], axis=0).astype(BF16)
            update = contract(left, right, TN)
            for g in range(first + tall, groups):
                if g not in after:
                    block[g] = block[g] - update[8 * g : 8 * g + 8, :BLK]
                inverse[g] = inverse[g] - update[8 * g : 8 * g + 8, BLK:]


SPAN = 4


def chol_kernel(
    fly,
    sub,
    place_ref,
    ridge_ref,
    gram_ref,
    out_ref,
    a_ref,
    l_ref,
    s_ref,
    d_ref,
    u_ref,
    inv_ref,
    sems,
):
    share, columns = out_ref.shape
    blocks = columns // BLK
    piece = a_ref.shape[0] // (fly * sub)
    stride = piece * fly
    wide = SPAN * BLK
    spans = blocks // SPAN

    def start(i, _):
        s, f = i // fly, i % fly
        pltpu.make_async_copy(
            gram_ref.at[f * sub + s, pl.ds(0, piece)],
            a_ref.at[pl.ds(pl.multiple_of(i * piece, 8), piece)],
            sems.at[s],
        ).start()
        return 0

    lax.fori_loop(0, fly * sub, start, 0)
    arrived = set()
    sub_i = lax.broadcasted_iota(jnp.int32, (BLK, BLK), 0)
    lane_i = lax.broadcasted_iota(jnp.int32, (BLK, BLK), 1)
    eye = jnp.where(sub_i == lane_i, ridge_ref[0], 0.0)

    def offset(k):
        other = blocks - 1 - k
        return k * stride if k < sub else other * stride + (blocks - other) * BLK

    def part(rows, col, which):
        return l_ref[rows, 2 * col + which * BLK : 2 * col + (which + 1) * BLK]

    def highs(rows, first, last):
        return jnp.concatenate([part(rows, c, 0) for c in range(first, last, BLK)], axis=1)

    def doubled(rows, first, last, which):
        pieces = [part(rows, c, which) for c in range(first, last, BLK)]
        return jnp.concatenate([p for piece in pieces for p in (piece, piece)], axis=1)

    def folded(value):
        return value[:, :BLK] + value[:, BLK:]

    def split(value):
        return jnp.concatenate(halves(value), axis=1)

    def solver(slot):
        pieces = [jnp.concatenate([w, w], axis=1) for w in halves(inv_ref[slot])]
        return jnp.concatenate(pieces, axis=0)

    def solve(rows, k, weights):
        lanes = slice(k % SPAN * BLK, (k % SPAN + 1) * BLK)
        low = folded(contract(split(s_ref[rows, lanes]), weights, NT))
        l_ref[rows, 2 * k * BLK : 2 * (k + 1) * BLK] = split(low)

    def widen(rows, q, span_high, span_rest):
        left = q * wide
        if q:
            both = l_ref[rows, : 2 * left]
            known = contract(both, span_high, NT) + contract(highs(rows, 0, left), span_rest, NT)
        for j in range(SPAN):
            k = q * SPAN + j
            skip = max(k * BLK - rows.start, 0)
            if skip >= rows.stop - rows.start:
                continue
            lanes = slice(j * BLK, (j + 1) * BLK)
            at = offset(k) + rows.start + skip - k * BLK
            value = a_ref[at : at + rows.stop - rows.start - skip, :]
            if q:
                value = value - known[skip:, lanes]
            s_ref[rows.start + skip : rows.stop, lanes] = value

    def pieces(first):
        return [slice(at, min(at + 2 * BLK, columns)) for at in range(first, columns, 2 * BLK)]

    for q in range(spans):
        left = q * wide
        for j in range(SPAN):
            k = q * SPAN + j
            owner = min(k, blocks - 1 - k)
            if owner not in arrived:
                arrived.add(owner)
                at = pl.ds(owner * stride, stride)
                pltpu.make_async_copy(a_ref.at[at], a_ref.at[at], sems.at[owner]).wait()
        span = slice(left, left + wide)
        span_high = span_rest = None
        if q:
            weights = solver((q * SPAN - 1) % 2)
            solve(span, q * SPAN - 1, weights)
            span_high = doubled(span, 0, left, 0)
            span_rest = jnp.concatenate([part(span, c, 1) for c in range(0, left, BLK)], axis=1)
        widen(span, q, span_high, span_rest)
        d_ref[...] = s_ref[left : left + BLK, :BLK] + eye
        for j in range(SPAN):
            k = q * SPAN + j
            top = k * BLK
            below = top + BLK
            lanes = slice(j * BLK, (j + 1) * BLK)
            mine = slice(top, below)
            if j == 0:
                work = pieces(left + wide)
                earlier = solver((k - 1) % 2) if q else None

                def step(rows):
                    if q:
                        solve(rows, k - 1, earlier)
                    widen(rows, q, span_high, span_rest)

            else:
                work = pieces(below)
                earlier = solver((k - 1) % 2)
                own = jnp.concatenate([doubled(mine, left, top, which) for which in range(2)], axis=0)

                def step(rows):
                    solve(rows, k - 1, earlier)
                    known = contract(l_ref[rows, 2 * left : 2 * top], own, NT)
                    s_ref[rows, lanes] = s_ref[rows, lanes] - folded(known)

            def between(t):
                if t < len(work):
                    step(work[t])

            factor(d_ref, u_ref, inv_ref.at[k % 2], between)
            l_ref[mine, 2 * top : 2 * below] = split(u_ref[...].T)
            if j < SPAN - 1:
                rows = slice(below, below + BLK)
                solve(rows, k, solver(k % 2))
                own = jnp.concatenate([doubled(rows, left, below, which) for which in range(2)], axis=0)
                known = folded(contract(l_ref[rows, 2 * left : 2 * below], own, NT))
                d_ref[...] = s_ref[rows, (j + 1) * BLK : (j + 2) * BLK] + eye - known
    mine = place_ref[0] * share
    at = pl.ds(pl.multiple_of(mine, share), share)
    row = lax.broadcasted_iota(jnp.int32, (share, BLK), 0) + mine
    col = lax.broadcasted_iota(jnp.int32, (share, BLK), 1)
    for c in range(0, columns, BLK):
        value = l_ref[at, 2 * c : 2 * c + BLK].astype(F32) + l_ref[at, 2 * c + BLK : 2 * c + 2 * BLK].astype(F32)
        out_ref[:, c : c + BLK] = jnp.where(col + c <= row, value, 0.0)


def factored(place, ridge, full, fly, sub, share):
    columns = share * fly * sub
    piece = (columns + BLK) // fly
    smem = pl.BlockSpec(memory_space=pltpu.SMEM)
    return pl.pallas_call(
        functools.partial(chol_kernel, fly, sub),
        out_shape=jax.ShapeDtypeStruct((share, columns), F32),
        in_specs=[smem, smem, pl.BlockSpec(memory_space=pl.ANY)],
        scratch_shapes=[
            pltpu.VMEM((piece * fly * sub, BLK), F32),
            pltpu.VMEM((columns, 2 * columns), BF16),
            pltpu.VMEM((columns, SPAN * BLK), F32),
            pltpu.VMEM((BLK, BLK), F32),
            pltpu.VMEM((BLK, BLK), F32),
            pltpu.VMEM((2, BLK, BLK), F32),
            pltpu.SemaphoreType.DMA((sub,)),
        ],
        compiler_params=pltpu.CompilerParams(vmem_limit_bytes=52 << 20),
        name="cholesky",
    )(place, ridge, full)


def across_kernel(x_ref, table_ref, local_ref, out_ref, norm_ref, mixed_ref):
    devices = table_ref.shape[0]
    length = x_ref.shape[1]
    here = x_ref.shape[0] // devices
    per = here - 8
    picks = out_ref.shape[0] * BLK // (per * devices)
    join = BLK // picks
    lanes = lax.broadcasted_iota(jnp.int32, VREG, 1)
    norms = jnp.zeros(VREG, F32)
    total = devices * length
    table, local = table_ref[...], local_ref[...]
    groups = devices // join
    owner = lax.broadcasted_iota(jnp.int32, (groups, BLK), 1) // picks

    def chosen(parts):
        out = parts[0]
        for j in range(1, join):
            out = jnp.where(owner == j, parts[j], out)
        return out

    numbers = []
    for j in range(join):
        value = x_ref[pl.ds(per + here * j, groups, stride=here * join), :]
        numbers.append(pltpu.roll(value, picks * j, 1) if j else value)
    index = chosen(numbers).astype(jnp.int32)

    def product(a, b):
        return sum(contract(*pair, NN) for pair in zip(a, b))

    for col in range(per):
        rows = x_ref[pl.ds(col, devices, stride=here), :]
        squares = jnp.sum(jnp.sum(rows * rows, axis=0, keepdims=True), axis=1, keepdims=True)
        norm = jnp.sqrt(jnp.broadcast_to(squares, VREG) / total + 1e-06)
        norms = jnp.where(lanes == col, norm, norms)
        scale = 1.0 / (norm[0:1, :] * math.sqrt(total))
        mixed = product([table] * 3, thirds(rows))
        mixed_ref[...] = product(thirds(mixed), [local] * 3) * scale
        taken = [
            jnp.take_along_axis(
                mixed_ref[pl.ds(j, groups, stride=join), :], index, axis=1, mode="promise_in_bounds"
            )
            for j in range(join)
        ]
        out_ref[pl.ds(col, groups, stride=per), :] = chosen(taken)
    norm_ref[...] = norms


def across(x, table, local, samples_all):
    devices = table.shape[0]
    per = x.shape[0] // devices - 8
    return pl.pallas_call(
        across_kernel,
        out_shape=[
            jax.ShapeDtypeStruct((samples_all * per // BLK, BLK), F32),
            jax.ShapeDtypeStruct(VREG, F32),
        ],
        scratch_shapes=[pltpu.VMEM((devices, BLK), F32)],
        compiler_params=pltpu.CompilerParams(vmem_limit_bytes=32 << 20),
        name="across_devices",
    )(x, table, local)


def gram_kernel(fly, per, sub_ref, *refs):
    parts, out_ref, high_ref, rest_ref = refs[:-3], refs[-3], refs[-2], refs[-1]
    sub = sub_ref[0]
    columns = high_ref.shape[0]
    blocks = columns // BLK
    depth = high_ref.shape[1] // BLK
    for i, ref in enumerate(parts):
        core = i // (len(parts) // 2)
        step = i % (len(parts) // 2) * 2
        source = (jnp.where(sub % 2 == 0, sub + core, sub - core) - step + len(parts)) % len(parts)
        for f in range(fly):
            at = pl.ds(pl.multiple_of((f * len(parts) + source) * per, per), per)
            for h in range(depth):
                row = (f * depth + h) * per
                high, rest = halves(ref[row : row + per, :])
                high_ref[at, h * BLK : (h + 1) * BLK] = high
                rest_ref[at, h * BLK : (h + 1) * BLK] = rest

    def block(index):
        at = pl.ds(pl.multiple_of(index * BLK, BLK), BLK)
        return high_ref[at, :], rest_ref[at, :]

    for j in range(blocks + 1):
        first = j < blocks - sub
        row = jnp.where(first, sub + j, j - 1)
        col = jnp.where(first, sub, blocks - 1 - sub)
        out_ref[j * BLK : (j + 1) * BLK, :] = contract_split(block(row), block(col), NT)


def gram_share(sub, parts, fly, per):
    columns = fly * len(parts) * per
    depth = parts[0].shape[0] // (fly * per) * BLK
    return pl.pallas_call(
        functools.partial(gram_kernel, fly, per),
        out_shape=jax.ShapeDtypeStruct((columns + BLK, BLK), F32),
        in_specs=[pl.BlockSpec(memory_space=pltpu.SMEM)]
        + [pl.BlockSpec(memory_space=pltpu.VMEM)] * len(parts),
        scratch_shapes=[pltpu.VMEM((columns, depth), BF16)] * 2,
        compiler_params=pltpu.CompilerParams(vmem_limit_bytes=32 << 20),
        name="gram_share",
    )(sub, *parts)


def shards(matrix, row_signs, sample_idx, ridge_shift):
    rows_here, columns = matrix.shape
    fly, sub = lax.axis_size("fly"), lax.axis_size("sub")
    devices = fly * sub
    place = lax.axis_index(AXES)
    samples = sample_idx.shape[0]
    samples_all = samples * devices
    per = columns // devices
    signed = (matrix * row_signs.astype(F32)[:, None]).T.reshape(devices, per, rows_here)
    numbers = jnp.zeros((8, rows_here), F32).at[0, :samples].set(sample_idx.astype(F32))
    numbers = jnp.broadcast_to(numbers[None], (devices, 8, rows_here))
    spread = lax.all_to_all(jnp.concatenate([signed, numbers], axis=1), AXES, 0, 0, tiled=True)
    table = jnp.asarray(sylvester(devices), BF16)
    local = jnp.asarray(sylvester(rows_here), BF16)
    picked, norms = across(spread.reshape(-1, rows_here), table, local, samples_all)
    mine = lax.all_to_all(picked.reshape(fly, -1, BLK), "fly", 0, 0, tiled=True).reshape(-1, BLK)
    parts = [mine]
    for step in range(2, sub, 2):
        parts.append(lax.ppermute(mine, "sub", [(i, (i + step) % sub) for i in range(sub)]))
    parts += [lax.ppermute(value, "sub", [(i, i ^ 1) for i in range(sub)]) for value in parts]
    share = gram_share(lax.axis_index("sub").astype(jnp.int32)[None], parts, fly, per)
    piece = (columns + BLK) // fly
    pieces = lax.all_to_all(share.reshape(fly, piece, BLK), "fly", 0, 0, tiled=True)
    summed = jnp.sum(pieces, axis=0) / samples_all
    full = lax.all_gather(jnp.concatenate([summed, norms], axis=0), AXES)
    chol = factored(place.astype(jnp.int32)[None], ridge_shift, full, fly, sub, per)
    col_norms = full[:, piece, :per].reshape(columns)
    return (chol, col_norms)


def solution(mesh):
    in_specs = (P(AXES, None), P(AXES), P(AXES), P())
    out_specs = (P(AXES, None), P())
    return jax.shard_map(shards, mesh=mesh, in_specs=in_specs, out_specs=out_specs, check_vma=False)
```

```python
import functools
import math

import jax
import jax.numpy as jnp
import numpy as np
from jax import lax
from jax.experimental import pallas as pl
from jax.experimental.pallas import tpu as pltpu
from jax.sharding import PartitionSpec as P

F32 = jnp.float32
BF16 = jnp.bfloat16
BLK = 128
VREG = (8, 128)
AXES = ("fly", "sub")


def sylvester(order):
    idx = np.arange(order)
    common = idx[:, None] & idx[None, :]
    parity = np.zeros((order, order), np.int64)
    for bit in range(order.bit_length() - 1):
        parity ^= common >> bit & 1
    return (1 - 2 * parity).astype(np.float32)


def halves(value):
    high = value.astype(BF16)
    return high, (value - high.astype(F32)).astype(BF16)


def thirds(value):
    high = value.astype(BF16)
    rest = value - high.astype(F32)
    mid = rest.astype(BF16)
    return high, mid, (rest - mid.astype(F32)).astype(BF16)


def contract(a, b, dims):
    return lax.dot_general(a, b, (dims, ((), ())), preferred_element_type=F32)


def contract_split(a, b, dims):
    return contract(a[0], b[0], dims) + (contract(a[0], b[1], dims) + contract(a[1], b[0], dims))


NT = ((1,), (1,))
TN = ((0,), (0,))
NN = ((1,), (0,))
WIDE = 16


def factor(d_ref, u_ref, inv_ref, splat_ref, between=None):
    steps, tall = BLK // WIDE, WIDE // 8
    sublane = lax.broadcasted_iota(jnp.int32, VREG, 0)
    lane = lax.broadcasted_iota(jnp.int32, VREG, 1)
    groups = BLK // 8
    block = [d_ref[8 * g : 8 * g + 8, :] for g in range(groups)]
    inverse = [jnp.where(lane == sublane + 8 * g, 1.0, 0.0).astype(F32) for g in range(groups)]

    def row(parts, i):
        part = parts[i // 8]
        return jnp.broadcast_to(part[i % 8 : i % 8 + 1, :], VREG)

    def total(terms):
        while len(terms) > 1:
            terms = [terms[i] + terms[i + 1] for i in range(0, len(terms), 2)]
        return terms[0]

    for t in range(steps):
        first = t * tall

        def column(g, c):
            at = WIDE * t + c
            return jnp.broadcast_to(block[g][:, at : at + 1], VREG)

        mine = range(first, first + tall)
        cols = [[column(g, c) for g in mine] for c in range(WIDE)]
        raw = [block[g] for g in mine]
        r, w = list(raw), [inverse[g] for g in mine]
        after = range(first + tall, min(first + 2 * tall, groups))
        for i in range(0, WIDE, 2):
            v, lo = i // 8, i % 8
            is_i, is_j = sublane == lo, sublane == lo + 1
            slot = 32 * (i // 2)
            for n in range(tall):
                splat_ref[slot + 8 * n : slot + 8 * n + 8, :] = cols[i][n]
                splat_ref[slot + 16 + 8 * n : slot + 24 + 8 * n, :] = cols[i + 1][n]

            def splat(j, m):
                at = slot + 16 * j + m
                return jnp.broadcast_to(splat_ref[at : at + 1, :], VREG)

            a, b, c = splat(0, i), splat(0, i + 1), splat(1, i + 1)
            det = a * c - b * b
            rdet = 1.0 / det
            ra = lax.rsqrt(a)
            l10 = b * ra
            rc = lax.rsqrt(det) * (a * ra)
            x = [c * p - b * q for p, q in zip(cols[i], cols[i + 1])]
            y = [a * q - b * p for p, q in zip(cols[i], cols[i + 1])]
            x[v] = jnp.where(is_i, det - c, jnp.where(is_j, b, x[v]))
            y[v] = jnp.where(is_i, b, jnp.where(is_j, det - a, y[v]))
            x, y = [p * rdet for p in x], [p * rdet for p in y]

            def sweep(parts, ri=None, rj=None):
                if ri is None:
                    ri, rj = row(parts, i), row(parts, i + 1)
                return [part - x[n] * ri - y[n] * rj for n, part in enumerate(parts)]

            for m in range(i + 2, WIDE):
                cols[m] = sweep(cols[m], splat(0, m), splat(1, m))
            at = WIDE * t + i
            for parts, ref in ((r, u_ref), (w, inv_ref)):
                ui = row(parts, i) * ra
                uj = (row(parts, i + 1) - l10 * ui) * rc
                ref[at : at + 1, :] = ui[0:1]
                ref[at + 1 : at + 2, :] = uj[0:1]
            r, w = sweep(r), sweep(w)
        if between is not None:
            between(t)
        if t == steps - 1:
            break
        ahead = {g: [column(g, c) for c in range(WIDE)] for g in after}
        q = [row(r, c) for c in range(WIDE)]
        for g in after:
            block[g] = block[g] - total([ahead[g][c] * q[c] for c in range(WIDE)])
        if True:
            xh, xm, xl = [p.astype(F32) for p in thirds(jnp.concatenate(raw, axis=0))]
            solved = jnp.concatenate([jnp.concatenate(r, axis=0), jnp.concatenate(w, axis=0)], axis=1)
            yh, ym, yl = [p.astype(F32) for p in thirds(solved)]
            left = jnp.concatenate([xh, xm, xh, xm, xl, xh], axis=0).astype(BF16)
            right = jnp.concatenate([yh, yh, ym, ym, yh, yl], axis=0).astype(BF16)
            update = contract(left, right, TN)
            for g in range(first + tall, groups):
                if g not in after:
                    block[g] = block[g] - update[8 * g : 8 * g + 8, :BLK]
                inverse[g] = inverse[g] - update[8 * g : 8 * g + 8, BLK:]


SPAN = 4


def chol_kernel(
    fly,
    sub,
    place_ref,
    ridge_ref,
    gram_ref,
    out_ref,
    norm_ref,
    a_ref,
    l_ref,
    s_ref,
    d_ref,
    u_ref,
    inv_ref,
    splat_ref,
    tile_ref,
    sems,
):
    share, columns = out_ref.shape
    blocks = columns // BLK
    piece = a_ref.shape[0] // (fly * sub)
    stride = piece * fly
    wide = SPAN * BLK
    spans = blocks // SPAN

    def start(i, _):
        s, f = i // fly, i % fly
        pltpu.make_async_copy(
            gram_ref.at[f * sub + s, pl.ds(0, piece)],
            a_ref.at[pl.ds(pl.multiple_of(i * piece, 8), piece)],
            sems.at[s],
        ).start()
        return 0

    lax.fori_loop(0, fly * sub, start, 0)
    norm_copy = pltpu.make_async_copy(gram_ref.at[:, pl.ds(piece, 8)], tile_ref, sems.at[sub])
    norm_copy.start()
    arrived = set()
    sub_i = lax.broadcasted_iota(jnp.int32, (BLK, BLK), 0)
    lane_i = lax.broadcasted_iota(jnp.int32, (BLK, BLK), 1)
    eye = jnp.where(sub_i == lane_i, ridge_ref[0], 0.0)

    def offset(k):
        other = blocks - 1 - k
        return k * stride if k < sub else other * stride + (blocks - other) * BLK

    def part(rows, col, which):
        return l_ref[rows, 2 * col + which * BLK : 2 * col + (which + 1) * BLK]

    def highs(rows, first, last):
        return jnp.concatenate([part(rows, c, 0) for c in range(first, last, BLK)], axis=1)

    def doubled(rows, first, last, which):
        pieces = [part(rows, c, which) for c in range(first, last, BLK)]
        return jnp.concatenate([p for piece in pieces for p in (piece, piece)], axis=1)

    def folded(value):
        return value[:, :BLK] + value[:, BLK:]

    def split(value):
        return jnp.concatenate(halves(value), axis=1)

    def solver(slot):
        pieces = [jnp.concatenate([w, w], axis=1) for w in halves(inv_ref[slot])]
        return jnp.concatenate(pieces, axis=0)

    def solve(rows, k, weights):
        lanes = slice(k % SPAN * BLK, (k % SPAN + 1) * BLK)
        low = folded(contract(split(s_ref[rows, lanes]), weights, NT))
        l_ref[rows, 2 * k * BLK : 2 * (k + 1) * BLK] = split(low)

    def widen(rows, q, span_high, span_rest):
        left = q * wide
        if q:
            both = l_ref[rows, : 2 * left]
            known = contract(both, span_high, NT) + contract(highs(rows, 0, left), span_rest, NT)
        for j in range(SPAN):
            k = q * SPAN + j
            skip = max(k * BLK - rows.start, 0)
            if skip >= rows.stop - rows.start:
                continue
            lanes = slice(j * BLK, (j + 1) * BLK)
            at = offset(k) + rows.start + skip - k * BLK
            value = a_ref[at : at + rows.stop - rows.start - skip, :]
            if q:
                value = value - known[skip:, lanes]
            s_ref[rows.start + skip : rows.stop, lanes] = value

    def pieces(first):
        return [slice(at, min(at + 2 * BLK, columns)) for at in range(first, columns, 2 * BLK)]

    for q in range(spans):
        left = q * wide
        for j in range(SPAN):
            k = q * SPAN + j
            owner = min(k, blocks - 1 - k)
            if owner not in arrived:
                arrived.add(owner)
                at = pl.ds(owner * stride, stride)
                pltpu.make_async_copy(a_ref.at[at], a_ref.at[at], sems.at[owner]).wait()
        span = slice(left, left + wide)
        span_high = span_rest = None
        if q:
            weights = solver((q * SPAN - 1) % 2)
            solve(span, q * SPAN - 1, weights)
            span_high = doubled(span, 0, left, 0)
            span_rest = jnp.concatenate([part(span, c, 1) for c in range(0, left, BLK)], axis=1)
        widen(span, q, span_high, span_rest)
        d_ref[...] = s_ref[left : left + BLK, :BLK] + eye
        for j in range(SPAN):
            k = q * SPAN + j
            top = k * BLK
            below = top + BLK
            lanes = slice(j * BLK, (j + 1) * BLK)
            mine = slice(top, below)
            if j == 0:
                work = pieces(left + wide)
                earlier = solver((k - 1) % 2) if q else None

                def step(rows):
                    if q:
                        solve(rows, k - 1, earlier)
                    widen(rows, q, span_high, span_rest)

            else:
                work = pieces(below)
                earlier = solver((k - 1) % 2)
                own = jnp.concatenate([doubled(mine, left, top, which) for which in range(2)], axis=0)

                def step(rows):
                    solve(rows, k - 1, earlier)
                    known = contract(l_ref[rows, 2 * left : 2 * top], own, NT)
                    s_ref[rows, lanes] = s_ref[rows, lanes] - folded(known)

            def between(t):
                if t < len(work):
                    step(work[t])

            factor(d_ref, u_ref, inv_ref.at[k % 2], splat_ref, between)
            l_ref[mine, 2 * top : 2 * below] = split(u_ref[...].T)
            if j < SPAN - 1:
                rows = slice(below, below + BLK)
                solve(rows, k, solver(k % 2))
                own = jnp.concatenate([doubled(rows, left, below, which) for which in range(2)], axis=0)
                known = folded(contract(l_ref[rows, 2 * left : 2 * below], own, NT))
                d_ref[...] = s_ref[rows, (j + 1) * BLK : (j + 2) * BLK] + eye - known
    norm_copy.wait()
    for g in range(norm_ref.shape[0]):
        members = range(g * BLK // share, (g + 1) * BLK // share)
        norm_ref[g : g + 1, :] = sum(tile_ref[i, 0:1, :] for i in members)
    mine = place_ref[0] * share
    at = pl.ds(pl.multiple_of(mine, share), share)
    row = lax.broadcasted_iota(jnp.int32, (share, BLK), 0) + mine
    col = lax.broadcasted_iota(jnp.int32, (share, BLK), 1)
    for c in range(0, columns, BLK):
        value = l_ref[at, 2 * c : 2 * c + BLK].astype(F32) + l_ref[at, 2 * c + BLK : 2 * c + 2 * BLK].astype(F32)
        out_ref[:, c : c + BLK] = jnp.where(col + c <= row, value, 0.0)


def factored(place, ridge, full, fly, sub, share):
    columns = share * fly * sub
    piece = (columns + BLK) // fly
    smem = pl.BlockSpec(memory_space=pltpu.SMEM)
    return pl.pallas_call(
        functools.partial(chol_kernel, fly, sub),
        out_shape=[
            jax.ShapeDtypeStruct((share, columns), F32),
            jax.ShapeDtypeStruct((columns // BLK, BLK), F32),
        ],
        in_specs=[smem, smem, pl.BlockSpec(memory_space=pl.ANY)],
        scratch_shapes=[
            pltpu.VMEM((piece * fly * sub, BLK), F32),
            pltpu.VMEM((columns, 2 * columns), BF16),
            pltpu.VMEM((columns, SPAN * BLK), F32),
            pltpu.VMEM((BLK, BLK), F32),
            pltpu.VMEM((BLK, BLK), F32),
            pltpu.VMEM((2, BLK, BLK), F32),
            pltpu.VMEM((272, BLK), F32),
            pltpu.VMEM((fly * sub, 8, BLK), F32),
            pltpu.SemaphoreType.DMA((sub + 1,)),
        ],
        compiler_params=pltpu.CompilerParams(vmem_limit_bytes=52 << 20),
        name="cholesky",
    )(place, ridge, full)


def across_kernel(slot_ref, x_ref, table_ref, local_ref, out_ref, norm_ref, mixed_ref):
    devices = table_ref.shape[0]
    length = x_ref.shape[1]
    here = x_ref.shape[0] // devices
    per = here - 8
    picks = out_ref.shape[0] * BLK // (per * devices)
    join = BLK // picks
    lanes = lax.broadcasted_iota(jnp.int32, VREG, 1)
    norms = jnp.zeros(VREG, F32)
    total = devices * length
    table, local = table_ref[...], local_ref[...]
    groups = devices // join
    owner = lax.broadcasted_iota(jnp.int32, (groups, BLK), 1) // picks

    def chosen(parts):
        out = parts[0]
        for j in range(1, join):
            out = jnp.where(owner == j, parts[j], out)
        return out

    numbers = []
    for j in range(join):
        value = x_ref[pl.ds(per + here * j, groups, stride=here * join), :]
        numbers.append(pltpu.roll(value, picks * j, 1) if j else value)
    index = chosen(numbers).astype(jnp.int32)

    def product(a, b):
        return sum(contract(*pair, NN) for pair in zip(a, b))

    for col in range(per):
        rows = x_ref[pl.ds(col, devices, stride=here), :]
        squares = jnp.sum(jnp.sum(rows * rows, axis=0, keepdims=True), axis=1, keepdims=True)
        norm = jnp.sqrt(jnp.broadcast_to(squares, VREG) / total + 1e-06)
        norms = jnp.where(lanes == col, norm, norms)
        scale = 1.0 / (norm[0:1, :] * math.sqrt(total))
        mixed = product([table] * 3, thirds(rows))
        mixed_ref[...] = product(thirds(mixed), [local] * 3) * scale
        taken = [
            jnp.take_along_axis(
                mixed_ref[pl.ds(j, groups, stride=join), :], index, axis=1, mode="promise_in_bounds"
            )
            for j in range(join)
        ]
        out_ref[pl.ds(col, groups, stride=per), :] = chosen(taken)
    norm_ref[...] = pltpu.roll(norms, slot_ref[0], 1)


def across(slot, x, table, local, samples_all):
    devices = table.shape[0]
    per = x.shape[0] // devices - 8
    return pl.pallas_call(
        across_kernel,
        out_shape=[
            jax.ShapeDtypeStruct((samples_all * per // BLK, BLK), F32),
            jax.ShapeDtypeStruct(VREG, F32),
        ],
        in_specs=[pl.BlockSpec(memory_space=pltpu.SMEM)] + [pl.BlockSpec(memory_space=pltpu.VMEM)] * 3,
        scratch_shapes=[pltpu.VMEM((devices, BLK), F32)],
        compiler_params=pltpu.CompilerParams(vmem_limit_bytes=32 << 20),
        name="across_devices",
    )(slot, x, table, local)


def gram_kernel(fly, per, sub_ref, *refs):
    parts, out_ref, high_ref, rest_ref = refs[:-3], refs[-3], refs[-2], refs[-1]
    sub = sub_ref[0]
    columns = high_ref.shape[0]
    blocks = columns // BLK
    depth = high_ref.shape[1] // BLK
    for i, ref in enumerate(parts):
        core = i // (len(parts) // 2)
        step = i % (len(parts) // 2) * 2
        source = (jnp.where(sub % 2 == 0, sub + core, sub - core) - step + len(parts)) % len(parts)
        for f in range(fly):
            at = pl.ds(pl.multiple_of((f * len(parts) + source) * per, per), per)
            for h in range(depth):
                row = (f * depth + h) * per
                high, rest = halves(ref[row : row + per, :])
                high_ref[at, h * BLK : (h + 1) * BLK] = high
                rest_ref[at, h * BLK : (h + 1) * BLK] = rest

    def block(index):
        at = pl.ds(pl.multiple_of(index * BLK, BLK), BLK)
        return high_ref[at, :], rest_ref[at, :]

    for j in range(blocks + 1):
        first = j < blocks - sub
        row = jnp.where(first, sub + j, j - 1)
        col = jnp.where(first, sub, blocks - 1 - sub)
        out_ref[j * BLK : (j + 1) * BLK, :] = contract_split(block(row), block(col), NT)


def gram_share(sub, parts, fly, per):
    columns = fly * len(parts) * per
    depth = parts[0].shape[0] // (fly * per) * BLK
    return pl.pallas_call(
        functools.partial(gram_kernel, fly, per),
        out_shape=jax.ShapeDtypeStruct((columns + BLK, BLK), F32),
        in_specs=[pl.BlockSpec(memory_space=pltpu.SMEM)]
        + [pl.BlockSpec(memory_space=pltpu.VMEM)] * len(parts),
        scratch_shapes=[pltpu.VMEM((columns, depth), BF16)] * 2,
        compiler_params=pltpu.CompilerParams(vmem_limit_bytes=32 << 20),
        name="gram_share",
    )(sub, *parts)


def shards(matrix, row_signs, sample_idx, ridge_shift):
    rows_here, columns = matrix.shape
    fly, sub = lax.axis_size("fly"), lax.axis_size("sub")
    devices = fly * sub
    place = lax.axis_index(AXES)
    samples = sample_idx.shape[0]
    samples_all = samples * devices
    per = columns // devices
    signed = (matrix * row_signs.astype(F32)[:, None]).T.reshape(devices, per, rows_here)
    numbers = jnp.zeros((8, rows_here), F32).at[0, :samples].set(sample_idx.astype(F32))
    numbers = jnp.broadcast_to(numbers[None], (devices, 8, rows_here))
    spread = lax.all_to_all(jnp.concatenate([signed, numbers], axis=1), AXES, 0, 0, tiled=True)
    table = jnp.asarray(sylvester(devices), BF16)
    local = jnp.asarray(sylvester(rows_here), BF16)
    slot = (place * per % BLK).astype(jnp.int32)[None]
    picked, norms = across(slot, spread.reshape(-1, rows_here), table, local, samples_all)
    mine = lax.all_to_all(picked.reshape(fly, -1, BLK), "fly", 0, 0, tiled=True).reshape(-1, BLK)
    parts = [mine]
    for step in range(2, sub, 2):
        parts.append(lax.ppermute(mine, "sub", [(i, (i + step) % sub) for i in range(sub)]))
    parts += [lax.ppermute(value, "sub", [(i, i ^ 1) for i in range(sub)]) for value in parts]
    share = gram_share(lax.axis_index("sub").astype(jnp.int32)[None], parts, fly, per)
    piece = (columns + BLK) // fly
    pieces = lax.all_to_all(share.reshape(fly, piece, BLK), "fly", 0, 0, tiled=True)
    summed = jnp.sum(pieces, axis=0) / samples_all
    full = lax.all_gather(jnp.concatenate([summed, norms], axis=0), AXES)
    chol, col_norms = factored(place.astype(jnp.int32)[None], ridge_shift, full, fly, sub, per)
    return (chol, col_norms.reshape(columns))


def solution(mesh):
    in_specs = (P(AXES, None), P(AXES), P(AXES), P())
    out_specs = (P(AXES, None), P())
    return jax.shard_map(shards, mesh=mesh, in_specs=in_specs, out_specs=out_specs, check_vma=False)
```

```python
import functools
import math

import jax
import jax.numpy as jnp
import numpy as np
from jax import lax
from jax.experimental import pallas as pl
from jax.experimental.pallas import tpu as pltpu
from jax.sharding import PartitionSpec as P

F32 = jnp.float32
BF16 = jnp.bfloat16
BLK = 128
VREG = (8, 128)
AXES = ("fly", "sub")


def sylvester(order):
    idx = np.arange(order)
    common = idx[:, None] & idx[None, :]
    parity = np.zeros((order, order), np.int64)
    for bit in range(order.bit_length() - 1):
        parity ^= common >> bit & 1
    return (1 - 2 * parity).astype(np.float32)


def halves(value):
    high = value.astype(BF16)
    return high, (value - high.astype(F32)).astype(BF16)


def thirds(value):
    high = value.astype(BF16)
    rest = value - high.astype(F32)
    mid = rest.astype(BF16)
    return high, mid, (rest - mid.astype(F32)).astype(BF16)


def contract(a, b, dims):
    return lax.dot_general(a, b, (dims, ((), ())), preferred_element_type=F32)


def contract_split(a, b, dims):
    return contract(a[0], b[0], dims) + (contract(a[0], b[1], dims) + contract(a[1], b[0], dims))


NT = ((1,), (1,))
TN = ((0,), (0,))
NN = ((1,), (0,))
WIDE = 16


def factor(d_ref, u_ref, inv_ref, splat_ref, between=None):
    steps, tall = BLK // WIDE, WIDE // 8
    sublane = lax.broadcasted_iota(jnp.int32, VREG, 0)
    lane = lax.broadcasted_iota(jnp.int32, VREG, 1)
    groups = BLK // 8
    block = [d_ref[8 * g : 8 * g + 8, :] for g in range(groups)]
    inverse = [jnp.where(lane == sublane + 8 * g, 1.0, 0.0).astype(F32) for g in range(groups)]

    def row(parts, i):
        part = parts[i // 8]
        return jnp.broadcast_to(part[i % 8 : i % 8 + 1, :], VREG)

    def total(terms):
        while len(terms) > 1:
            terms = [terms[i] + terms[i + 1] for i in range(0, len(terms), 2)]
        return terms[0]

    for t in range(steps):
        first = t * tall

        def column(g, c):
            at = WIDE * t + c
            return jnp.broadcast_to(block[g][:, at : at + 1], VREG)

        mine = range(first, first + tall)
        cols = [[column(g, c) for g in mine] for c in range(WIDE)]
        raw = [block[g] for g in mine]
        r, w = list(raw), [inverse[g] for g in mine]
        after = range(first + tall, min(first + 2 * tall, groups))
        for i in range(0, WIDE, 2):
            v, lo = i // 8, i % 8
            is_i, is_j = sublane == lo, sublane == lo + 1
            slot = 32 * (i // 2)
            for n in range(tall):
                splat_ref[slot + 8 * n : slot + 8 * n + 8, :] = cols[i][n]
                splat_ref[slot + 16 + 8 * n : slot + 24 + 8 * n, :] = cols[i + 1][n]

            def splat(j, m):
                at = slot + 16 * j + m
                return jnp.broadcast_to(splat_ref[at : at + 1, :], VREG)

            a, b, c = splat(0, i), splat(0, i + 1), splat(1, i + 1)
            det = a * c - b * b
            rdet = 1.0 / det
            ra = lax.rsqrt(a)
            l10 = b * ra
            rc = lax.rsqrt(det) * (a * ra)
            x = [c * p - b * q for p, q in zip(cols[i], cols[i + 1])]
            y = [a * q - b * p for p, q in zip(cols[i], cols[i + 1])]
            x[v] = jnp.where(is_i, det - c, jnp.where(is_j, b, x[v]))
            y[v] = jnp.where(is_i, b, jnp.where(is_j, det - a, y[v]))
            x, y = [p * rdet for p in x], [p * rdet for p in y]

            def sweep(parts, ri=None, rj=None):
                if ri is None:
                    ri, rj = row(parts, i), row(parts, i + 1)
                return [part - x[n] * ri - y[n] * rj for n, part in enumerate(parts)]

            for m in range(i + 2, WIDE):
                cols[m] = sweep(cols[m], splat(0, m), splat(1, m))
            at = WIDE * t + i
            for parts, ref in ((r, u_ref), (w, inv_ref)):
                ui = row(parts, i) * ra
                uj = (row(parts, i + 1) - l10 * ui) * rc
                ref[at : at + 1, :] = ui[0:1]
                ref[at + 1 : at + 2, :] = uj[0:1]
            r, w = sweep(r), sweep(w)
        if between is not None:
            between(t)
        if t == steps - 1:
            break
        ahead = {g: [column(g, c) for c in range(WIDE)] for g in after}
        q = [row(r, c) for c in range(WIDE)]
        for g in after:
            block[g] = block[g] - total([ahead[g][c] * q[c] for c in range(WIDE)])
        if True:
            xh, xm, xl = [p.astype(F32) for p in thirds(jnp.concatenate(raw, axis=0))]
            solved = jnp.concatenate([jnp.concatenate(r, axis=0), jnp.concatenate(w, axis=0)], axis=1)
            yh, ym, yl = [p.astype(F32) for p in thirds(solved)]
            left = jnp.concatenate([xh, xm, xh, xm, xl, xh], axis=0).astype(BF16)
            right = jnp.concatenate([yh, yh, ym, ym, yh, yl], axis=0).astype(BF16)
            update = contract(left, right, TN)
            for g in range(first + tall, groups):
                if g not in after:
                    block[g] = block[g] - update[8 * g : 8 * g + 8, :BLK]
                inverse[g] = inverse[g] - update[8 * g : 8 * g + 8, BLK:]


SPAN = 4


def spread_rows(blocks, first, last, sub):
    found = [(i, k) for k in range(first, last) for i in range(k, blocks)]
    return found + [found[-1]] * (-len(found) % sub)


def panels(first, last, place_ref, ridge_ref, arrive, a_ref, l_ref, s_ref, d_ref, u_ref, inv_ref, splat_ref):
    columns = l_ref.shape[0]
    blocks = columns // BLK
    wide = SPAN * BLK
    sub_i = lax.broadcasted_iota(jnp.int32, (BLK, BLK), 0)
    lane_i = lax.broadcasted_iota(jnp.int32, (BLK, BLK), 1)
    eye = jnp.where(sub_i == lane_i, ridge_ref[0], 0.0)

    def offset(k):
        return sum(blocks - i for i in range(first * SPAN, k)) * BLK

    def part(rows, col, which):
        return l_ref[rows, 2 * col + which * BLK : 2 * col + (which + 1) * BLK]

    def highs(rows, first, last):
        return jnp.concatenate([part(rows, c, 0) for c in range(first, last, BLK)], axis=1)

    def doubled(rows, first, last, which):
        pieces = [part(rows, c, which) for c in range(first, last, BLK)]
        return jnp.concatenate([p for piece in pieces for p in (piece, piece)], axis=1)

    def folded(value):
        return value[:, :BLK] + value[:, BLK:]

    def split(value):
        return jnp.concatenate(halves(value), axis=1)

    def solver(slot):
        pieces = [jnp.concatenate([w, w], axis=1) for w in halves(inv_ref[slot])]
        return jnp.concatenate(pieces, axis=0)

    def solve(rows, k, weights):
        lanes = slice(k % SPAN * BLK, (k % SPAN + 1) * BLK)
        low = folded(contract(split(s_ref[rows, lanes]), weights, NT))
        l_ref[rows, 2 * k * BLK : 2 * (k + 1) * BLK] = split(low)

    def widen(rows, q, span_high, span_rest):
        left = q * wide
        if q:
            both = l_ref[rows, : 2 * left]
            known = contract(both, span_high, NT) + contract(highs(rows, 0, left), span_rest, NT)
        for j in range(SPAN):
            k = q * SPAN + j
            skip = max(k * BLK - rows.start, 0)
            if skip >= rows.stop - rows.start:
                continue
            lanes = slice(j * BLK, (j + 1) * BLK)
            at = offset(k) + rows.start + skip - k * BLK
            value = a_ref[at : at + rows.stop - rows.start - skip, :]
            if q:
                value = value - known[skip:, lanes]
            s_ref[rows.start + skip : rows.stop, lanes] = value

    def pieces(first):
        return [slice(at, min(at + 2 * BLK, columns)) for at in range(first, columns, 2 * BLK)]

    for q in range(first, last):
        left = q * wide
        arrive(q)
        span = slice(left, left + wide)
        span_high = span_rest = None
        if q:
            if q > first:
                solve(span, q * SPAN - 1, solver((q * SPAN - 1) % 2))
            span_high = doubled(span, 0, left, 0)
            span_rest = jnp.concatenate([part(span, c, 1) for c in range(0, left, BLK)], axis=1)
        widen(span, q, span_high, span_rest)
        d_ref[...] = s_ref[left : left + BLK, :BLK] + eye
        for j in range(SPAN):
            k = q * SPAN + j
            top = k * BLK
            below = top + BLK
            lanes = slice(j * BLK, (j + 1) * BLK)
            mine = slice(top, below)
            if j == 0:
                work = pieces(left + wide)
                earlier = solver((k - 1) % 2) if q > first else None

                def step(rows):
                    if q > first:
                        solve(rows, k - 1, earlier)
                    widen(rows, q, span_high, span_rest)

            else:
                work = pieces(below)
                earlier = solver((k - 1) % 2)
                own = jnp.concatenate([doubled(mine, left, top, which) for which in range(2)], axis=0)

                def step(rows):
                    solve(rows, k - 1, earlier)
                    known = contract(l_ref[rows, 2 * left : 2 * top], own, NT)
                    s_ref[rows, lanes] = s_ref[rows, lanes] - folded(known)

            def between(t):
                if t < len(work):
                    step(work[t])

            factor(d_ref, u_ref, inv_ref.at[k % 2], splat_ref, between)
            l_ref[mine, 2 * top : 2 * below] = split(u_ref[...].T)
            if j < SPAN - 1:
                rows = slice(below, below + BLK)
                solve(rows, k, solver(k % 2))
                own = jnp.concatenate([doubled(rows, left, below, which) for which in range(2)], axis=0)
                known = folded(contract(l_ref[rows, 2 * left : 2 * below], own, NT))
                d_ref[...] = s_ref[rows, (j + 1) * BLK : (j + 2) * BLK] + eye - known
    if last * SPAN < blocks:
        weights = solver((last * SPAN - 1) % 2)
        for rows in pieces(last * wide):
            solve(rows, last * SPAN - 1, weights)


def near_kernel(fly, sub, place_ref, ridge_ref, own_ref, other_ref, l_ref, a_ref, *rest):
    *scratch, sem = rest
    piece = a_ref.shape[0] // (fly * sub)
    hops = sub // 2
    me = place_ref[0] % sub
    sibling = me + 1 - 2 * (me % 2)

    def start(i, _):
        f, hop = i // hops, i % hops
        for ref, base in ((own_ref, me), (other_ref, sibling)):
            source = (base - 2 * hop + sub) % sub
            at = pl.ds(pl.multiple_of((source * fly + f) * piece, 8), piece)
            pltpu.make_async_copy(ref.at[f, hop], a_ref.at[at], sem).start()
        return 0

    lax.fori_loop(0, fly * hops, start, 0)

    def arrive(_):
        pltpu.make_async_copy(a_ref, a_ref, sem).wait()

    panels(0, 1, place_ref, ridge_ref, arrive, a_ref, l_ref, *scratch)


def chol_kernel(fly, sub, place_ref, ridge_ref, gram_ref, near_ref, out_ref, norm_ref, a_ref, l_ref, *rest):
    *scratch, tile_ref, sems = rest
    share, columns = out_ref.shape
    blocks = columns // BLK
    piece = a_ref.shape[0] // (fly * sub)
    stride = piece * fly
    spans = blocks // SPAN

    def start(i, _):
        s, f = i // fly, i % fly
        pltpu.make_async_copy(
            gram_ref.at[f * sub + s, pl.ds(0, piece)],
            a_ref.at[pl.ds(pl.multiple_of(i * piece, 8), piece)],
            sems.at[s],
        ).start()
        return 0

    known = near_ref.shape[1]
    near_copy = pltpu.make_async_copy(near_ref, l_ref.at[:, pl.ds(0, known)], sems.at[sub + 1])
    near_copy.start()
    lax.fori_loop(0, fly * sub, start, 0)
    norm_copy = pltpu.make_async_copy(gram_ref.at[:, pl.ds(piece, 8)], tile_ref, sems.at[sub])
    norm_copy.start()
    near_copy.wait()
    arrived = set()

    def arrive(q):
        end = sum(blocks - i for i in range(SPAN, (q + 1) * SPAN)) * BLK
        for s in range(min(pl.cdiv(end, stride), sub)):
            if s not in arrived:
                arrived.add(s)
                at = pl.ds(s * stride, stride)
                pltpu.make_async_copy(a_ref.at[at], a_ref.at[at], sems.at[s]).wait()

    panels(1, spans, place_ref, ridge_ref, arrive, a_ref, l_ref, *scratch)
    for s in range(sub):
        if s not in arrived:
            at = pl.ds(s * stride, stride)
            pltpu.make_async_copy(a_ref.at[at], a_ref.at[at], sems.at[s]).wait()
    norm_copy.wait()
    for g in range(norm_ref.shape[0]):
        members = range(g * BLK // share, (g + 1) * BLK // share)
        norm_ref[g : g + 1, :] = sum(tile_ref[i, 0:1, :] for i in members)
    mine = place_ref[0] * share
    at = pl.ds(pl.multiple_of(mine, share), share)
    row = lax.broadcasted_iota(jnp.int32, (share, BLK), 0) + mine
    col = lax.broadcasted_iota(jnp.int32, (share, BLK), 1)
    for c in range(0, columns, BLK):
        value = l_ref[at, 2 * c : 2 * c + BLK].astype(F32) + l_ref[at, 2 * c + BLK : 2 * c + 2 * BLK].astype(F32)
        out_ref[:, c : c + BLK] = jnp.where(col + c <= row, value, 0.0)


def chol_scratch(columns):
    return [
        pltpu.VMEM((columns, SPAN * BLK), F32),
        pltpu.VMEM((BLK, BLK), F32),
        pltpu.VMEM((BLK, BLK), F32),
        pltpu.VMEM((2, BLK, BLK), F32),
        pltpu.VMEM((272, BLK), F32),
    ]


def factored_near(place, ridge, own, other, fly, sub, columns):
    smem, hbm = pl.BlockSpec(memory_space=pltpu.SMEM), pl.BlockSpec(memory_space=pl.ANY)
    rows = len(spread_rows(columns // BLK, 0, SPAN, sub)) * BLK
    return pl.pallas_call(
        functools.partial(near_kernel, fly, sub),
        out_shape=jax.ShapeDtypeStruct((columns, 2 * SPAN * BLK), BF16),
        in_specs=[smem, smem, hbm, hbm],
        scratch_shapes=[pltpu.VMEM((rows, BLK), F32)] + chol_scratch(columns) + [pltpu.SemaphoreType.DMA],
        compiler_params=pltpu.CompilerParams(vmem_limit_bytes=52 << 20),
        cost_estimate=pl.CostEstimate(flops=16 * 10**9, bytes_accessed=8 * 10**6, transcendentals=0),
        name="cholesky_first",
    )(place, ridge, own, other)


def factored(place, ridge, full, near, fly, sub, share):
    columns = share * fly * sub
    smem, hbm = pl.BlockSpec(memory_space=pltpu.SMEM), pl.BlockSpec(memory_space=pl.ANY)
    rows = len(spread_rows(columns // BLK, SPAN, columns // BLK, sub)) * BLK
    return pl.pallas_call(
        functools.partial(chol_kernel, fly, sub),
        out_shape=[
            jax.ShapeDtypeStruct((share, columns), F32),
            jax.ShapeDtypeStruct((columns // BLK, BLK), F32),
        ],
        in_specs=[smem, smem, hbm, hbm],
        scratch_shapes=[pltpu.VMEM((rows, BLK), F32), pltpu.VMEM((columns, 2 * columns), BF16)]
        + chol_scratch(columns)
        + [pltpu.VMEM((fly * sub, 8, BLK), F32), pltpu.SemaphoreType.DMA((sub + 2,))],
        compiler_params=pltpu.CompilerParams(vmem_limit_bytes=52 << 20),
        name="cholesky_rest",
    )(place, ridge, full, near)


def across_kernel(slot_ref, x_ref, table_ref, local_ref, out_ref, norm_ref, mixed_ref):
    devices = table_ref.shape[0]
    length = x_ref.shape[1]
    here = x_ref.shape[0] // devices
    per = here - 8
    picks = out_ref.shape[0] * BLK // (per * devices)
    join = BLK // picks
    lanes = lax.broadcasted_iota(jnp.int32, VREG, 1)
    norms = jnp.zeros(VREG, F32)
    total = devices * length
    table, local = table_ref[...], local_ref[...]
    groups = devices // join
    owner = lax.broadcasted_iota(jnp.int32, (groups, BLK), 1) // picks

    def chosen(parts):
        out = parts[0]
        for j in range(1, join):
            out = jnp.where(owner == j, parts[j], out)
        return out

    numbers = []
    for j in range(join):
        value = x_ref[pl.ds(per + here * j, groups, stride=here * join), :]
        numbers.append(pltpu.roll(value, picks * j, 1) if j else value)
    index = chosen(numbers).astype(jnp.int32)

    def product(a, b):
        return sum(contract(*pair, NN) for pair in zip(a, b))

    for col in range(per):
        rows = x_ref[pl.ds(col, devices, stride=here), :]
        squares = jnp.sum(jnp.sum(rows * rows, axis=0, keepdims=True), axis=1, keepdims=True)
        norm = jnp.sqrt(jnp.broadcast_to(squares, VREG) / total + 1e-06)
        norms = jnp.where(lanes == col, norm, norms)
        scale = 1.0 / (norm[0:1, :] * math.sqrt(total))
        mixed = product([table] * 3, thirds(rows))
        mixed_ref[...] = product(thirds(mixed), [local] * 3) * scale
        taken = [
            jnp.take_along_axis(
                mixed_ref[pl.ds(j, groups, stride=join), :], index, axis=1, mode="promise_in_bounds"
            )
            for j in range(join)
        ]
        out_ref[pl.ds(col, groups, stride=per), :] = chosen(taken)
    norm_ref[...] = pltpu.roll(norms, slot_ref[0], 1)


def across(slot, x, table, local, samples_all):
    devices = table.shape[0]
    per = x.shape[0] // devices - 8
    return pl.pallas_call(
        across_kernel,
        out_shape=[
            jax.ShapeDtypeStruct((samples_all * per // BLK, BLK), F32),
            jax.ShapeDtypeStruct(VREG, F32),
        ],
        in_specs=[pl.BlockSpec(memory_space=pltpu.SMEM)] + [pl.BlockSpec(memory_space=pltpu.VMEM)] * 3,
        scratch_shapes=[pltpu.VMEM((devices, BLK), F32)],
        compiler_params=pltpu.CompilerParams(vmem_limit_bytes=32 << 20),
        name="across_devices",
    )(slot, x, table, local)


def gram_kernel(fly, per, sizes, sub_ref, table_ref, *refs):
    parts, out_ref, high_ref, rest_ref = refs[:-3], refs[-3], refs[-2], refs[-1]
    sub = sub_ref[0]
    columns = high_ref.shape[0]
    blocks = columns // BLK
    depth = high_ref.shape[1] // BLK
    for i, ref in enumerate(parts):
        core = i // (len(parts) // 2)
        step = i % (len(parts) // 2) * 2
        source = (jnp.where(sub % 2 == 0, sub + core, sub - core) - step + len(parts)) % len(parts)
        for f in range(fly):
            at = pl.ds(pl.multiple_of((f * len(parts) + source) * per, per), per)
            for h in range(depth):
                row = (f * depth + h) * per
                high, rest = halves(ref[row : row + per, :])
                high_ref[at, h * BLK : (h + 1) * BLK] = high
                rest_ref[at, h * BLK : (h + 1) * BLK] = rest

    def block(index):
        at = pl.ds(pl.multiple_of(index * BLK, BLK), BLK)
        return high_ref[at, :], rest_ref[at, :]

    counts = [size * fly // BLK for size in sizes]
    start = 0
    for n, size in enumerate(sizes):
        for j in range(counts[n]):
            entry = 2 * (sub * sum(counts) + sum(counts[:n]) + j)
            value = contract_split(block(table_ref[entry]), block(table_ref[entry + 1]), NT)
            row = j * BLK
            while row < (j + 1) * BLK:
                f, inside = row // size, row % size
                many = min(size - inside, (j + 1) * BLK - row)
                at = f * sum(sizes) + start + inside
                out_ref[at : at + many, :] = value[row - j * BLK : row - j * BLK + many]
                row += many
        start += size


def gram_share(sub, parts, fly, per, lists):
    each = [len(found) // len(parts) for found in lists]
    table = [entry for s in range(len(parts)) for n, found in zip(each, lists) for entry in found[s * n : (s + 1) * n]]
    sizes = [n * BLK // fly for n in each]
    columns = fly * len(parts) * per
    depth = parts[0].shape[0] // (fly * per) * BLK
    return pl.pallas_call(
        functools.partial(gram_kernel, fly, per, sizes),
        out_shape=jax.ShapeDtypeStruct((sum(each) * BLK, BLK), F32),
        in_specs=[pl.BlockSpec(memory_space=pltpu.SMEM)] * 2
        + [pl.BlockSpec(memory_space=pltpu.VMEM)] * len(parts),
        scratch_shapes=[pltpu.VMEM((columns, depth), BF16)] * 2,
        compiler_params=pltpu.CompilerParams(vmem_limit_bytes=32 << 20),
        name="gram_share",
    )(sub, jnp.asarray(np.array(table, np.int32).reshape(-1)), *parts)


def shards(matrix, row_signs, sample_idx, ridge_shift):
    rows_here, columns = matrix.shape
    fly, sub = lax.axis_size("fly"), lax.axis_size("sub")
    devices = fly * sub
    place = lax.axis_index(AXES)
    samples = sample_idx.shape[0]
    samples_all = samples * devices
    per = columns // devices
    signed = (matrix * row_signs.astype(F32)[:, None]).T.reshape(devices, per, rows_here)
    numbers = jnp.zeros((8, rows_here), F32).at[0, :samples].set(sample_idx.astype(F32))
    numbers = jnp.broadcast_to(numbers[None], (devices, 8, rows_here))
    spread = lax.all_to_all(jnp.concatenate([signed, numbers], axis=1), AXES, 0, 0, tiled=True)
    table = jnp.asarray(sylvester(devices), BF16)
    local = jnp.asarray(sylvester(rows_here), BF16)
    slot = (place * per % BLK).astype(jnp.int32)[None]
    picked, norms = across(slot, spread.reshape(-1, rows_here), table, local, samples_all)
    mine = lax.all_to_all(picked.reshape(fly, -1, BLK), "fly", 0, 0, tiled=True).reshape(-1, BLK)
    parts = [mine]
    for step in range(2, sub, 2):
        parts.append(lax.ppermute(mine, "sub", [(i, (i + step) % sub) for i in range(sub)]))
    parts += [lax.ppermute(value, "sub", [(i, i ^ 1) for i in range(sub)]) for value in parts]
    blocks = columns // BLK
    lists = [spread_rows(blocks, 0, SPAN, sub), spread_rows(blocks, SPAN, blocks, sub)]
    share = gram_share(lax.axis_index("sub").astype(jnp.int32)[None], parts, fly, per, lists)
    pieces = lax.all_to_all(share.reshape(fly, -1, BLK), "fly", 0, 0, tiled=True)
    summed = jnp.sum(pieces, axis=0) / samples_all
    size = len(lists[0]) // sub * BLK // fly
    full = lax.all_gather(jnp.concatenate([summed[size:], norms], axis=0), AXES)
    near = [summed[:size]]
    for step in range(2, sub, 2):
        near.append(lax.ppermute(near[0], "sub", [(i, (i + step) % sub) for i in range(sub)]))
    near = jnp.broadcast_to(jnp.stack(near)[None], (fly, sub // 2, size, BLK))
    own = lax.all_to_all(near, "fly", 0, 0, tiled=True)
    other = lax.ppermute(own, "sub", [(i, i ^ 1) for i in range(sub)])
    index = place.astype(jnp.int32)[None]
    first = factored_near(index, ridge_shift, own, other, fly, sub, columns)
    chol, col_norms = factored(index, ridge_shift, full, first, fly, sub, per)
    return (chol, col_norms.reshape(columns))


def solution(mesh):
    in_specs = (P(AXES, None), P(AXES), P(AXES), P())
    out_specs = (P(AXES, None), P())
    return jax.shard_map(shards, mesh=mesh, in_specs=in_specs, out_specs=out_specs, check_vma=False)
```

```python
import functools
import math

import jax
import jax.numpy as jnp
import numpy as np
from jax import lax
from jax.experimental import pallas as pl
from jax.experimental.pallas import tpu as pltpu
from jax.sharding import PartitionSpec as P

F32 = jnp.float32
BF16 = jnp.bfloat16
BLK = 128
VREG = (8, 128)
AXES = ("fly", "sub")


def sylvester(order):
    idx = np.arange(order)
    common = idx[:, None] & idx[None, :]
    parity = np.zeros((order, order), np.int64)
    for bit in range(order.bit_length() - 1):
        parity ^= common >> bit & 1
    return (1 - 2 * parity).astype(np.float32)


def halves(value):
    high = value.astype(BF16)
    return high, (value - high.astype(F32)).astype(BF16)


def thirds(value):
    high = value.astype(BF16)
    rest = value - high.astype(F32)
    mid = rest.astype(BF16)
    return high, mid, (rest - mid.astype(F32)).astype(BF16)


def contract(a, b, dims):
    return lax.dot_general(a, b, (dims, ((), ())), preferred_element_type=F32)


def contract_split(a, b, dims):
    return contract(a[0], b[0], dims) + (contract(a[0], b[1], dims) + contract(a[1], b[0], dims))


NT = ((1,), (1,))
TN = ((0,), (0,))
NN = ((1,), (0,))
WIDE = 16


def factor(d_ref, u_ref, inv_ref, splat_ref, between=None):
    steps, tall = BLK // WIDE, WIDE // 8
    sublane = lax.broadcasted_iota(jnp.int32, VREG, 0)
    lane = lax.broadcasted_iota(jnp.int32, VREG, 1)
    groups = BLK // 8
    block = [d_ref[8 * g : 8 * g + 8, :] for g in range(groups)]
    inverse = [jnp.where(lane == sublane + 8 * g, 1.0, 0.0).astype(F32) for g in range(groups)]

    def row(parts, i):
        part = parts[i // 8]
        return jnp.broadcast_to(part[i % 8 : i % 8 + 1, :], VREG)

    def total(terms):
        while len(terms) > 1:
            terms = [terms[i] + terms[i + 1] for i in range(0, len(terms), 2)]
        return terms[0]

    for t in range(steps):
        first = t * tall

        def column(g, c):
            at = WIDE * t + c
            return jnp.broadcast_to(block[g][:, at : at + 1], VREG)

        mine = range(first, first + tall)
        cols = [[column(g, c) for g in mine] for c in range(WIDE)]
        raw = [block[g] for g in mine]
        r, w = list(raw), [inverse[g] for g in mine]
        after = range(first + tall, min(first + 2 * tall, groups))
        for i in range(0, WIDE, 2):
            v, lo = i // 8, i % 8
            is_i, is_j = sublane == lo, sublane == lo + 1
            slot = 32 * (i // 2)
            for n in range(tall):
                splat_ref[slot + 8 * n : slot + 8 * n + 8, :] = cols[i][n]
                splat_ref[slot + 16 + 8 * n : slot + 24 + 8 * n, :] = cols[i + 1][n]

            def splat(j, m):
                at = slot + 16 * j + m
                return jnp.broadcast_to(splat_ref[at : at + 1, :], VREG)

            a, b, c = splat(0, i), splat(0, i + 1), splat(1, i + 1)
            det = a * c - b * b
            rdet = 1.0 / det
            ra = lax.rsqrt(a)
            l10 = b * ra
            rc = lax.rsqrt(det) * (a * ra)
            x = [c * p - b * q for p, q in zip(cols[i], cols[i + 1])]
            y = [a * q - b * p for p, q in zip(cols[i], cols[i + 1])]
            x[v] = jnp.where(is_i, det - c, jnp.where(is_j, b, x[v]))
            y[v] = jnp.where(is_i, b, jnp.where(is_j, det - a, y[v]))
            x, y = [p * rdet for p in x], [p * rdet for p in y]

            def sweep(parts, ri=None, rj=None):
                if ri is None:
                    ri, rj = row(parts, i), row(parts, i + 1)
                return [part - x[n] * ri - y[n] * rj for n, part in enumerate(parts)]

            for m in range(i + 2, WIDE):
                cols[m] = sweep(cols[m], splat(0, m), splat(1, m))
            at = WIDE * t + i
            for parts, ref in ((r, u_ref), (w, inv_ref)):
                ui = row(parts, i) * ra
                uj = (row(parts, i + 1) - l10 * ui) * rc
                ref[at : at + 1, :] = ui[0:1]
                ref[at + 1 : at + 2, :] = uj[0:1]
            r, w = sweep(r), sweep(w)
        if between is not None:
            between(t)
        if t == steps - 1:
            break
        ahead = {g: [column(g, c) for c in range(WIDE)] for g in after}
        q = [row(r, c) for c in range(WIDE)]
        for g in after:
            block[g] = block[g] - total([ahead[g][c] * q[c] for c in range(WIDE)])
        if True:
            xh, xm, xl = [p.astype(F32) for p in thirds(jnp.concatenate(raw, axis=0))]
            solved = jnp.concatenate([jnp.concatenate(r, axis=0), jnp.concatenate(w, axis=0)], axis=1)
            yh, ym, yl = [p.astype(F32) for p in thirds(solved)]
            left = jnp.concatenate([xh, xm, xh, xm, xl, xh], axis=0).astype(BF16)
            right = jnp.concatenate([yh, yh, ym, ym, yh, yl], axis=0).astype(BF16)
            update = contract(left, right, TN)
            for g in range(first + tall, groups):
                if g not in after:
                    block[g] = block[g] - update[8 * g : 8 * g + 8, :BLK]
                inverse[g] = inverse[g] - update[8 * g : 8 * g + 8, BLK:]


NEAR = 5
SPAN = 4


def span_starts(blocks):
    return [0] + list(range(NEAR, blocks, SPAN)) + [blocks]


def spread_rows(blocks, first, last, sub):
    found = [(i, k) for k in range(first, last) for i in range(k, blocks)]
    return found + [found[-1]] * (-len(found) % sub)


def panels(first, last, place_ref, ridge_ref, arrive, a_ref, l_ref, s_ref, d_ref, u_ref, inv_ref, splat_ref, ahead_ref):
    columns = l_ref.shape[0]
    blocks = columns // BLK
    starts = span_starts(blocks)
    sub_i = lax.broadcasted_iota(jnp.int32, (BLK, BLK), 0)
    lane_i = lax.broadcasted_iota(jnp.int32, (BLK, BLK), 1)
    eye = jnp.where(sub_i == lane_i, ridge_ref[0], 0.0)

    def offset(k):
        return sum(blocks - i for i in range(starts[first], k)) * BLK

    def part(rows, col, which):
        return l_ref[rows, 2 * col + which * BLK : 2 * col + (which + 1) * BLK]

    def highs(rows, first, last):
        return jnp.concatenate([part(rows, c, 0) for c in range(first, last, BLK)], axis=1)

    def doubled(rows, first, last, which):
        pieces = [part(rows, c, which) for c in range(first, last, BLK)]
        return jnp.concatenate([p for piece in pieces for p in (piece, piece)], axis=1)

    def folded(value):
        return value[:, :BLK] + value[:, BLK:]

    def split(value):
        return jnp.concatenate(halves(value), axis=1)

    def solver(slot):
        pieces = [jnp.concatenate([w, w], axis=1) for w in halves(inv_ref[slot])]
        return jnp.concatenate(pieces, axis=0)

    def solve(rows, k, weights):
        j = k - max(start for start in starts if start <= k)
        lanes = slice(j * BLK, (j + 1) * BLK)
        low = folded(contract(split(s_ref[rows, lanes]), weights, NT))
        l_ref[rows, 2 * k * BLK : 2 * (k + 1) * BLK] = split(low)

    def weights_of(span, low, left):
        rests = [part(span, c, 1) for c in range(low, left, BLK)]
        return doubled(span, low, left, 0), jnp.concatenate(rests, axis=1)

    def product(rows, low, left, weights):
        known = contract(l_ref[rows, 2 * low : 2 * left], weights[0], NT)
        return known + contract(highs(rows, low, left), weights[1], NT)

    def widen(rows, q, weights, low=0, base=None):
        left = starts[q] * BLK
        if q:
            known = product(rows, low, left, weights)
            if base is not None:
                known = known + base
        for j in range(starts[q + 1] - starts[q]):
            k = starts[q] + j
            skip = max(k * BLK - rows.start, 0)
            if skip >= rows.stop - rows.start:
                continue
            lanes = slice(j * BLK, (j + 1) * BLK)
            at = offset(k) + rows.start + skip - k * BLK
            value = a_ref[at : at + rows.stop - rows.start - skip, :]
            if q:
                value = value - known[skip:, lanes]
            s_ref[rows.start + skip : rows.stop, lanes] = value

    def pieces(first):
        return [slice(at, min(at + 2 * BLK, columns)) for at in range(first, columns, 2 * BLK)]

    for q in range(first, last):
        left, wide = starts[q] * BLK, (starts[q + 1] - starts[q]) * BLK
        arrive(q)
        span = slice(left, left + wide)
        full = None
        if q:
            if q > first:
                solve(span, starts[q] - 1, solver((starts[q] - 1) % 2))
            full = weights_of(span, 0, left)
        if q > max(first, 1):
            low = starts[q - 1] * BLK
            widen(span, q, weights_of(span, low, left), low, ahead_ref[:wide, :wide])
        else:
            widen(span, q, full)
        d_ref[...] = s_ref[left : left + BLK, :BLK] + eye
        for j in range(starts[q + 1] - starts[q]):
            k = starts[q] + j
            top = k * BLK
            below = top + BLK
            lanes = slice(j * BLK, (j + 1) * BLK)
            mine = slice(top, below)
            if j == 0:
                work = pieces(left + wide)
                earlier = solver((k - 1) % 2) if q > first else None

                def step(rows):
                    if q > first:
                        solve(rows, k - 1, earlier)
                    widen(rows, q, full)

            else:
                work = pieces(below)
                earlier = solver((k - 1) % 2)
                own = jnp.concatenate([doubled(mine, left, top, which) for which in range(2)], axis=0)

                def step(rows):
                    solve(rows, k - 1, earlier)
                    known = contract(l_ref[rows, 2 * left : 2 * top], own, NT)
                    s_ref[rows, lanes] = s_ref[rows, lanes] - folded(known)

            def between(t):
                if t < len(work):
                    step(work[t])
                elif t == BLK // WIDE - 2 and q and q + 1 < last and j in (1, 2):
                    begin, end = (starts[q + 1] * BLK, starts[q + 2] * BLK)
                    middle = begin + (starts[q + 2] - starts[q + 1]) // 2 * BLK
                    rows = (slice(begin, middle), slice(middle, end))[j - 1]
                    coming = weights_of(slice(begin, end), 0, left)
                    value = product(rows, 0, left, coming)
                    ahead_ref[rows.start - begin : rows.stop - begin, : end - begin] = value

            factor(d_ref, u_ref, inv_ref.at[k % 2], splat_ref, between)
            l_ref[mine, 2 * top : 2 * below] = split(u_ref[...].T)
            if k < starts[q + 1] - 1:
                rows = slice(below, below + BLK)
                solve(rows, k, solver(k % 2))
                own = jnp.concatenate([doubled(rows, left, below, which) for which in range(2)], axis=0)
                known = folded(contract(l_ref[rows, 2 * left : 2 * below], own, NT))
                d_ref[...] = s_ref[rows, (j + 1) * BLK : (j + 2) * BLK] + eye - known
    if starts[last] < blocks:
        weights = solver((starts[last] - 1) % 2)
        for rows in pieces(starts[last] * BLK):
            solve(rows, starts[last] - 1, weights)


def near_kernel(fly, sub, place_ref, ridge_ref, own_ref, other_ref, l_ref, a_ref, *rest):
    *scratch, sem = rest
    piece = a_ref.shape[0] // (fly * sub)
    hops = sub // 2
    me = place_ref[0] % sub
    sibling = me + 1 - 2 * (me % 2)

    def start(i, _):
        f, hop = i // hops, i % hops
        for ref, base in ((own_ref, me), (other_ref, sibling)):
            source = (base - 2 * hop + sub) % sub
            at = pl.ds(pl.multiple_of((source * fly + f) * piece, 8), piece)
            pltpu.make_async_copy(ref.at[f, hop], a_ref.at[at], sem).start()
        return 0

    lax.fori_loop(0, fly * hops, start, 0)

    def arrive(_):
        pltpu.make_async_copy(a_ref, a_ref, sem).wait()

    panels(0, 1, place_ref, ridge_ref, arrive, a_ref, l_ref, *scratch)


def chol_kernel(fly, sub, place_ref, ridge_ref, gram_ref, near_ref, out_ref, norm_ref, a_ref, l_ref, *rest):
    *scratch, tile_ref, sems = rest
    share, columns = out_ref.shape
    blocks = columns // BLK
    piece = a_ref.shape[0] // (fly * sub)
    stride = piece * fly
    starts = span_starts(blocks)
    spans = len(starts) - 1

    def start(i, _):
        s, f = i // fly, i % fly
        pltpu.make_async_copy(
            gram_ref.at[f * sub + s, pl.ds(0, piece)],
            a_ref.at[pl.ds(pl.multiple_of(i * piece, 8), piece)],
            sems.at[s],
        ).start()
        return 0

    known = near_ref.shape[1]
    near_copy = pltpu.make_async_copy(near_ref, l_ref.at[:, pl.ds(0, known)], sems.at[sub + 1])
    near_copy.start()
    lax.fori_loop(0, fly * sub, start, 0)
    norm_copy = pltpu.make_async_copy(gram_ref.at[:, pl.ds(piece, 8)], tile_ref, sems.at[sub])
    norm_copy.start()
    near_copy.wait()
    arrived = set()

    def arrive(q):
        end = sum(blocks - i for i in range(NEAR, starts[q + 1])) * BLK
        for s in range(min(pl.cdiv(end, stride), sub)):
            if s not in arrived:
                arrived.add(s)
                at = pl.ds(s * stride, stride)
                pltpu.make_async_copy(a_ref.at[at], a_ref.at[at], sems.at[s]).wait()

    panels(1, spans, place_ref, ridge_ref, arrive, a_ref, l_ref, *scratch)
    for s in range(sub):
        if s not in arrived:
            at = pl.ds(s * stride, stride)
            pltpu.make_async_copy(a_ref.at[at], a_ref.at[at], sems.at[s]).wait()
    norm_copy.wait()
    for g in range(norm_ref.shape[0]):
        members = range(g * BLK // share, (g + 1) * BLK // share)
        norm_ref[g : g + 1, :] = sum(tile_ref[i, 0:1, :] for i in members)
    mine = place_ref[0] * share
    at = pl.ds(pl.multiple_of(mine, share), share)
    row = lax.broadcasted_iota(jnp.int32, (share, BLK), 0) + mine
    col = lax.broadcasted_iota(jnp.int32, (share, BLK), 1)
    for c in range(0, columns, BLK):
        value = l_ref[at, 2 * c : 2 * c + BLK].astype(F32) + l_ref[at, 2 * c + BLK : 2 * c + 2 * BLK].astype(F32)
        out_ref[:, c : c + BLK] = jnp.where(col + c <= row, value, 0.0)


def chol_scratch(columns):
    return [
        pltpu.VMEM((columns, max(NEAR, SPAN) * BLK), F32),
        pltpu.VMEM((BLK, BLK), F32),
        pltpu.VMEM((BLK, BLK), F32),
        pltpu.VMEM((2, BLK, BLK), F32),
        pltpu.VMEM((272, BLK), F32),
        pltpu.VMEM((SPAN * BLK, SPAN * BLK), F32),
    ]


def factored_near(place, ridge, own, other, fly, sub, columns):
    smem, hbm = pl.BlockSpec(memory_space=pltpu.SMEM), pl.BlockSpec(memory_space=pl.ANY)
    rows = len(spread_rows(columns // BLK, 0, NEAR, sub)) * BLK
    return pl.pallas_call(
        functools.partial(near_kernel, fly, sub),
        out_shape=jax.ShapeDtypeStruct((columns, 2 * NEAR * BLK), BF16),
        in_specs=[smem, smem, hbm, hbm],
        scratch_shapes=[pltpu.VMEM((rows, BLK), F32)] + chol_scratch(columns) + [pltpu.SemaphoreType.DMA],
        compiler_params=pltpu.CompilerParams(vmem_limit_bytes=52 << 20),
        cost_estimate=pl.CostEstimate(flops=16 * 10**9, bytes_accessed=8 * 10**6, transcendentals=0),
        name="cholesky_first",
    )(place, ridge, own, other)


def factored(place, ridge, full, near, fly, sub, share):
    columns = share * fly * sub
    smem, hbm = pl.BlockSpec(memory_space=pltpu.SMEM), pl.BlockSpec(memory_space=pl.ANY)
    rows = len(spread_rows(columns // BLK, NEAR, columns // BLK, sub)) * BLK
    return pl.pallas_call(
        functools.partial(chol_kernel, fly, sub),
        out_shape=[
            jax.ShapeDtypeStruct((share, columns), F32),
            jax.ShapeDtypeStruct((columns // BLK, BLK), F32),
        ],
        in_specs=[smem, smem, hbm, hbm],
        scratch_shapes=[pltpu.VMEM((rows, BLK), F32), pltpu.VMEM((columns, 2 * columns), BF16)]
        + chol_scratch(columns)
        + [pltpu.VMEM((fly * sub, 8, BLK), F32), pltpu.SemaphoreType.DMA((sub + 2,))],
        compiler_params=pltpu.CompilerParams(vmem_limit_bytes=52 << 20),
        name="cholesky_rest",
    )(place, ridge, full, near)


def across_kernel(slot_ref, x_ref, table_ref, local_ref, out_ref, norm_ref, mixed_ref):
    devices = table_ref.shape[0]
    length = x_ref.shape[1]
    here = x_ref.shape[0] // devices
    per = here - 8
    picks = out_ref.shape[0] * BLK // (per * devices)
    join = BLK // picks
    lanes = lax.broadcasted_iota(jnp.int32, VREG, 1)
    norms = jnp.zeros(VREG, F32)
    total = devices * length
    table, local = table_ref[...], local_ref[...]
    groups = devices // join
    owner = lax.broadcasted_iota(jnp.int32, (groups, BLK), 1) // picks

    def chosen(parts):
        out = parts[0]
        for j in range(1, join):
            out = jnp.where(owner == j, parts[j], out)
        return out

    numbers = []
    for j in range(join):
        value = x_ref[pl.ds(per + here * j, groups, stride=here * join), :]
        numbers.append(pltpu.roll(value, picks * j, 1) if j else value)
    index = chosen(numbers).astype(jnp.int32)

    def product(a, b):
        return sum(contract(*pair, NN) for pair in zip(a, b))

    for col in range(per):
        rows = x_ref[pl.ds(col, devices, stride=here), :]
        squares = jnp.sum(jnp.sum(rows * rows, axis=0, keepdims=True), axis=1, keepdims=True)
        norm = jnp.sqrt(jnp.broadcast_to(squares, VREG) / total + 1e-06)
        norms = jnp.where(lanes == col, norm, norms)
        scale = 1.0 / (norm[0:1, :] * math.sqrt(total))
        mixed = product([table] * 3, thirds(rows))
        mixed_ref[...] = product(thirds(mixed), [local] * 3) * scale
        taken = [
            jnp.take_along_axis(
                mixed_ref[pl.ds(j, groups, stride=join), :], index, axis=1, mode="promise_in_bounds"
            )
            for j in range(join)
        ]
        out_ref[pl.ds(col, groups, stride=per), :] = chosen(taken)
    norm_ref[...] = pltpu.roll(norms, slot_ref[0], 1)


def across(slot, x, table, local, samples_all):
    devices = table.shape[0]
    per = x.shape[0] // devices - 8
    return pl.pallas_call(
        across_kernel,
        out_shape=[
            jax.ShapeDtypeStruct((samples_all * per // BLK, BLK), F32),
            jax.ShapeDtypeStruct(VREG, F32),
        ],
        in_specs=[pl.BlockSpec(memory_space=pltpu.SMEM)] + [pl.BlockSpec(memory_space=pltpu.VMEM)] * 3,
        scratch_shapes=[pltpu.VMEM((devices, BLK), F32)],
        compiler_params=pltpu.CompilerParams(vmem_limit_bytes=32 << 20),
        name="across_devices",
    )(slot, x, table, local)


def gram_kernel(fly, per, sizes, sub_ref, table_ref, *refs):
    parts, out_ref, high_ref, rest_ref = refs[:-3], refs[-3], refs[-2], refs[-1]
    sub = sub_ref[0]
    columns = high_ref.shape[0]
    blocks = columns // BLK
    depth = high_ref.shape[1] // BLK
    for i, ref in enumerate(parts):
        core = i // (len(parts) // 2)
        step = i % (len(parts) // 2) * 2
        source = (jnp.where(sub % 2 == 0, sub + core, sub - core) - step + len(parts)) % len(parts)
        for f in range(fly):
            at = pl.ds(pl.multiple_of((f * len(parts) + source) * per, per), per)
            for h in range(depth):
                row = (f * depth + h) * per
                high, rest = halves(ref[row : row + per, :])
                high_ref[at, h * BLK : (h + 1) * BLK] = high
                rest_ref[at, h * BLK : (h + 1) * BLK] = rest

    def block(index):
        at = pl.ds(pl.multiple_of(index * BLK, BLK), BLK)
        return high_ref[at, :], rest_ref[at, :]

    counts = [size * fly // BLK for size in sizes]
    start = 0
    for n, size in enumerate(sizes):
        for j in range(counts[n]):
            entry = 2 * (sub * sum(counts) + sum(counts[:n]) + j)
            value = contract_split(block(table_ref[entry]), block(table_ref[entry + 1]), NT)
            row = j * BLK
            while row < (j + 1) * BLK:
                f, inside = row // size, row % size
                many = min(size - inside, (j + 1) * BLK - row)
                at = f * sum(sizes) + start + inside
                out_ref[at : at + many, :] = value[row - j * BLK : row - j * BLK + many]
                row += many
        start += size


def gram_share(sub, parts, fly, per, lists):
    each = [len(found) // len(parts) for found in lists]
    table = [entry for s in range(len(parts)) for n, found in zip(each, lists) for entry in found[s * n : (s + 1) * n]]
    sizes = [n * BLK // fly for n in each]
    columns = fly * len(parts) * per
    depth = parts[0].shape[0] // (fly * per) * BLK
    return pl.pallas_call(
        functools.partial(gram_kernel, fly, per, sizes),
        out_shape=jax.ShapeDtypeStruct((sum(each) * BLK, BLK), F32),
        in_specs=[pl.BlockSpec(memory_space=pltpu.SMEM)] * 2
        + [pl.BlockSpec(memory_space=pltpu.VMEM)] * len(parts),
        scratch_shapes=[pltpu.VMEM((columns, depth), BF16)] * 2,
        compiler_params=pltpu.CompilerParams(vmem_limit_bytes=32 << 20),
        name="gram_share",
    )(sub, jnp.asarray(np.array(table, np.int32).reshape(-1)), *parts)


def shards(matrix, row_signs, sample_idx, ridge_shift):
    rows_here, columns = matrix.shape
    fly, sub = lax.axis_size("fly"), lax.axis_size("sub")
    devices = fly * sub
    place = lax.axis_index(AXES)
    samples = sample_idx.shape[0]
    samples_all = samples * devices
    per = columns // devices
    signed = (matrix * row_signs.astype(F32)[:, None]).T.reshape(devices, per, rows_here)
    numbers = jnp.zeros((8, rows_here), F32).at[0, :samples].set(sample_idx.astype(F32))
    numbers = jnp.broadcast_to(numbers[None], (devices, 8, rows_here))
    spread = lax.all_to_all(jnp.concatenate([signed, numbers], axis=1), AXES, 0, 0, tiled=True)
    table = jnp.asarray(sylvester(devices), BF16)
    local = jnp.asarray(sylvester(rows_here), BF16)
    slot = (place * per % BLK).astype(jnp.int32)[None]
    picked, norms = across(slot, spread.reshape(-1, rows_here), table, local, samples_all)
    mine = lax.all_to_all(picked.reshape(fly, -1, BLK), "fly", 0, 0, tiled=True).reshape(-1, BLK)
    parts = [mine]
    for step in range(2, sub, 2):
        parts.append(lax.ppermute(mine, "sub", [(i, (i + step) % sub) for i in range(sub)]))
    parts += [lax.ppermute(value, "sub", [(i, i ^ 1) for i in range(sub)]) for value in parts]
    blocks = columns // BLK
    lists = [spread_rows(blocks, 0, NEAR, sub), spread_rows(blocks, NEAR, blocks, sub)]
    share = gram_share(lax.axis_index("sub").astype(jnp.int32)[None], parts, fly, per, lists)
    pieces = lax.all_to_all(share.reshape(fly, -1, BLK), "fly", 0, 0, tiled=True)
    summed = jnp.sum(pieces, axis=0) / samples_all
    size = len(lists[0]) // sub * BLK // fly
    full = lax.all_gather(jnp.concatenate([summed[size:], norms], axis=0), AXES)
    near = [summed[:size]]
    for step in range(2, sub, 2):
        near.append(lax.ppermute(near[0], "sub", [(i, (i + step) % sub) for i in range(sub)]))
    near = jnp.broadcast_to(jnp.stack(near)[None], (fly, sub // 2, size, BLK))
    own = lax.all_to_all(near, "fly", 0, 0, tiled=True)
    other = lax.ppermute(own, "sub", [(i, i ^ 1) for i in range(sub)])
    index = place.astype(jnp.int32)[None]
    first = factored_near(index, ridge_shift, own, other, fly, sub, columns)
    chol, col_norms = factored(index, ridge_shift, full, first, fly, sub, per)
    return (chol, col_norms.reshape(columns))


def solution(mesh):
    in_specs = (P(AXES, None), P(AXES), P(AXES), P())
    out_specs = (P(AXES, None), P())
    return jax.shard_map(shards, mesh=mesh, in_specs=in_specs, out_specs=out_specs, check_vma=False)
```

```python
import functools
import math

import jax
import jax.numpy as jnp
import numpy as np
from jax import lax
from jax.experimental import pallas as pl
from jax.experimental.pallas import tpu as pltpu
from jax.sharding import PartitionSpec as P

F32 = jnp.float32
BF16 = jnp.bfloat16
BLK = 128
VREG = (8, 128)
AXES = ("fly", "sub")


def sylvester(order):
    idx = np.arange(order)
    common = idx[:, None] & idx[None, :]
    parity = np.zeros((order, order), np.int64)
    for bit in range(order.bit_length() - 1):
        parity ^= common >> bit & 1
    return (1 - 2 * parity).astype(np.float32)


def halves(value):
    high = value.astype(BF16)
    return high, (value - high.astype(F32)).astype(BF16)


def thirds(value):
    high = value.astype(BF16)
    rest = value - high.astype(F32)
    mid = rest.astype(BF16)
    return high, mid, (rest - mid.astype(F32)).astype(BF16)


def contract(a, b, dims):
    return lax.dot_general(a, b, (dims, ((), ())), preferred_element_type=F32)


def contract_split(a, b, dims):
    return contract(a[0], b[0], dims) + (contract(a[0], b[1], dims) + contract(a[1], b[0], dims))


NT = ((1,), (1,))
TN = ((0,), (0,))
NN = ((1,), (0,))
WIDE = 16


def factor(d_ref, u_ref, inv_ref, splat_ref, between=None):
    steps, tall = BLK // WIDE, WIDE // 8
    sublane = lax.broadcasted_iota(jnp.int32, VREG, 0)
    lane = lax.broadcasted_iota(jnp.int32, VREG, 1)
    groups = BLK // 8
    block = [d_ref[8 * g : 8 * g + 8, :] for g in range(groups)]
    inverse = [jnp.where(lane == sublane + 8 * g, 1.0, 0.0).astype(F32) for g in range(groups)]

    def row(parts, i):
        part = parts[i // 8]
        return jnp.broadcast_to(part[i % 8 : i % 8 + 1, :], VREG)

    def total(terms):
        while len(terms) > 1:
            terms = [terms[i] + terms[i + 1] for i in range(0, len(terms), 2)]
        return terms[0]

    for t in range(steps):
        first = t * tall

        def column(g, c):
            at = WIDE * t + c
            return jnp.broadcast_to(block[g][:, at : at + 1], VREG)

        mine = range(first, first + tall)
        cols = [[column(g, c) for g in mine] for c in range(WIDE)]
        raw = [block[g] for g in mine]
        r, w = list(raw), [inverse[g] for g in mine]
        after = range(first + tall, min(first + 2 * tall, groups))
        for i in range(0, WIDE, 2):
            v, lo = i // 8, i % 8
            is_i, is_j = sublane == lo, sublane == lo + 1
            slot = 32 * (i // 2)
            for n in range(tall):
                splat_ref[slot + 8 * n : slot + 8 * n + 8, :] = cols[i][n]
                splat_ref[slot + 16 + 8 * n : slot + 24 + 8 * n, :] = cols[i + 1][n]

            def splat(j, m):
                at = slot + 16 * j + m
                return jnp.broadcast_to(splat_ref[at : at + 1, :], VREG)

            a, b, c = splat(0, i), splat(0, i + 1), splat(1, i + 1)
            det = a * c - b * b
            rdet = 1.0 / det
            ra = lax.rsqrt(a)
            l10 = b * ra
            rc = lax.rsqrt(det) * (a * ra)
            x = [c * p - b * q for p, q in zip(cols[i], cols[i + 1])]
            y = [a * q - b * p for p, q in zip(cols[i], cols[i + 1])]
            x[v] = jnp.where(is_i, det - c, jnp.where(is_j, b, x[v]))
            y[v] = jnp.where(is_i, b, jnp.where(is_j, det - a, y[v]))
            x, y = [p * rdet for p in x], [p * rdet for p in y]

            def sweep(parts, ri=None, rj=None):
                if ri is None:
                    ri, rj = row(parts, i), row(parts, i + 1)
                return [part - x[n] * ri - y[n] * rj for n, part in enumerate(parts)]

            for m in range(i + 2, WIDE):
                cols[m] = sweep(cols[m], splat(0, m), splat(1, m))
            at = WIDE * t + i
            for parts, ref in ((r, u_ref), (w, inv_ref)):
                ui = row(parts, i) * ra
                uj = (row(parts, i + 1) - l10 * ui) * rc
                ref[at : at + 1, :] = ui[0:1]
                ref[at + 1 : at + 2, :] = uj[0:1]
            r, w = sweep(r), sweep(w)
        if between is not None:
            between(t)
        if t == steps - 1:
            break
        ahead = {g: [column(g, c) for c in range(WIDE)] for g in after}
        q = [row(r, c) for c in range(WIDE)]
        for g in after:
            block[g] = block[g] - total([ahead[g][c] * q[c] for c in range(WIDE)])
        if True:
            xh, xm, xl = [p.astype(F32) for p in thirds(jnp.concatenate(raw, axis=0))]
            solved = jnp.concatenate([jnp.concatenate(r, axis=0), jnp.concatenate(w, axis=0)], axis=1)
            yh, ym, yl = [p.astype(F32) for p in thirds(solved)]
            left = jnp.concatenate([xh, xm, xh, xm, xl, xh], axis=0).astype(BF16)
            right = jnp.concatenate([yh, yh, ym, ym, yh, yl], axis=0).astype(BF16)
            update = contract(left, right, TN)
            for g in range(first + tall, groups):
                if g not in after:
                    block[g] = block[g] - update[8 * g : 8 * g + 8, :BLK]
                inverse[g] = inverse[g] - update[8 * g : 8 * g + 8, BLK:]


NEAR = 6
SPAN = 4


def span_starts(blocks):
    return [0] + list(range(NEAR, blocks, SPAN)) + [blocks]


def spread_rows(blocks, first, last, sub):
    found = [(i, k) for k in range(first, last) for i in range(k, blocks)]
    return found + [found[-1]] * (-len(found) % sub)


def panels(first, last, place_ref, ridge_ref, arrive, a_ref, l_ref, s_ref, d_ref, u_ref, inv_ref, splat_ref, ahead_ref):
    columns = l_ref.shape[0]
    blocks = columns // BLK
    starts = span_starts(blocks)
    sub_i = lax.broadcasted_iota(jnp.int32, (BLK, BLK), 0)
    lane_i = lax.broadcasted_iota(jnp.int32, (BLK, BLK), 1)
    eye = jnp.where(sub_i == lane_i, ridge_ref[0], 0.0)

    def offset(k):
        return sum(blocks - i for i in range(starts[first], k)) * BLK

    def part(rows, col, which):
        return l_ref[rows, 2 * col + which * BLK : 2 * col + (which + 1) * BLK]

    def highs(rows, first, last):
        return jnp.concatenate([part(rows, c, 0) for c in range(first, last, BLK)], axis=1)

    def doubled(rows, first, last, which):
        pieces = [part(rows, c, which) for c in range(first, last, BLK)]
        return jnp.concatenate([p for piece in pieces for p in (piece, piece)], axis=1)

    def folded(value):
        return value[:, :BLK] + value[:, BLK:]

    def split(value):
        return jnp.concatenate(halves(value), axis=1)

    def solver(slot):
        pieces = [jnp.concatenate([w, w], axis=1) for w in halves(inv_ref[slot])]
        return jnp.concatenate(pieces, axis=0)

    def solve(rows, k, weights):
        j = k - max(start for start in starts if start <= k)
        lanes = slice(j * BLK, (j + 1) * BLK)
        low = folded(contract(split(s_ref[rows, lanes]), weights, NT))
        l_ref[rows, 2 * k * BLK : 2 * (k + 1) * BLK] = split(low)

    def weights_of(span, low, left):
        rests = [part(span, c, 1) for c in range(low, left, BLK)]
        return doubled(span, low, left, 0), jnp.concatenate(rests, axis=1)

    def product(rows, low, left, weights):
        known = contract(l_ref[rows, 2 * low : 2 * left], weights[0], NT)
        return known + contract(highs(rows, low, left), weights[1], NT)

    def widen(rows, q, weights, low=0, base=None):
        left = starts[q] * BLK
        if q:
            known = product(rows, low, left, weights)
            if base is not None:
                known = known + base
        for j in range(starts[q + 1] - starts[q]):
            k = starts[q] + j
            skip = max(k * BLK - rows.start, 0)
            if skip >= rows.stop - rows.start:
                continue
            lanes = slice(j * BLK, (j + 1) * BLK)
            at = offset(k) + rows.start + skip - k * BLK
            value = a_ref[at : at + rows.stop - rows.start - skip, :]
            if q:
                value = value - known[skip:, lanes]
            s_ref[rows.start + skip : rows.stop, lanes] = value

    def pieces(first):
        return [slice(at, min(at + 2 * BLK, columns)) for at in range(first, columns, 2 * BLK)]

    for q in range(first, last):
        left, wide = starts[q] * BLK, (starts[q + 1] - starts[q]) * BLK
        arrive(q)
        span = slice(left, left + wide)
        full = None
        if q:
            if q > first:
                solve(span, starts[q] - 1, solver((starts[q] - 1) % 2))
            full = weights_of(span, 0, left)
        if q > max(first, 1):
            low = starts[q - 1] * BLK
            widen(span, q, weights_of(span, low, left), low, ahead_ref[:wide, :wide])
        else:
            widen(span, q, full)
        d_ref[...] = s_ref[left : left + BLK, :BLK] + eye
        for j in range(starts[q + 1] - starts[q]):
            k = starts[q] + j
            top = k * BLK
            below = top + BLK
            lanes = slice(j * BLK, (j + 1) * BLK)
            mine = slice(top, below)
            if j == 0:
                work = pieces(left + wide)
                earlier = solver((k - 1) % 2) if q > first else None

                def step(rows):
                    if q > first:
                        solve(rows, k - 1, earlier)
                    widen(rows, q, full)

            else:
                work = pieces(below)
                earlier = solver((k - 1) % 2)
                own = jnp.concatenate([doubled(mine, left, top, which) for which in range(2)], axis=0)

                def step(rows):
                    solve(rows, k - 1, earlier)
                    known = contract(l_ref[rows, 2 * left : 2 * top], own, NT)
                    s_ref[rows, lanes] = s_ref[rows, lanes] - folded(known)

            def between(t):
                if t < len(work):
                    step(work[t])
                elif t == BLK // WIDE - 2 and q and q + 1 < last and j in (1, 2):
                    begin, end = (starts[q + 1] * BLK, starts[q + 2] * BLK)
                    middle = begin + (starts[q + 2] - starts[q + 1]) // 2 * BLK
                    rows = (slice(begin, middle), slice(middle, end))[j - 1]
                    coming = weights_of(slice(begin, end), 0, left)
                    value = product(rows, 0, left, coming)
                    ahead_ref[rows.start - begin : rows.stop - begin, : end - begin] = value

            factor(d_ref, u_ref, inv_ref.at[k % 2], splat_ref, between)
            l_ref[mine, 2 * top : 2 * below] = split(u_ref[...].T)
            if k < starts[q + 1] - 1:
                rows = slice(below, below + BLK)
                solve(rows, k, solver(k % 2))
                own = jnp.concatenate([doubled(rows, left, below, which) for which in range(2)], axis=0)
                known = folded(contract(l_ref[rows, 2 * left : 2 * below], own, NT))
                d_ref[...] = s_ref[rows, (j + 1) * BLK : (j + 2) * BLK] + eye - known
    if starts[last] < blocks:
        weights = solver((starts[last] - 1) % 2)
        for rows in pieces(starts[last] * BLK):
            solve(rows, starts[last] - 1, weights)


def near_kernel(fly, sub, place_ref, ridge_ref, own_ref, other_ref, l_ref, a_ref, *rest):
    *scratch, sem = rest
    piece = a_ref.shape[0] // (fly * sub)
    hops = sub // 2
    me = place_ref[0] % sub
    sibling = me + 1 - 2 * (me % 2)

    def start(i, _):
        f, hop = i // hops, i % hops
        for ref, base in ((own_ref, me), (other_ref, sibling)):
            source = (base - 2 * hop + sub) % sub
            at = pl.ds(pl.multiple_of((source * fly + f) * piece, 8), piece)
            pltpu.make_async_copy(ref.at[f, hop], a_ref.at[at], sem).start()
        return 0

    lax.fori_loop(0, fly * hops, start, 0)

    def arrive(_):
        pltpu.make_async_copy(a_ref, a_ref, sem).wait()

    panels(0, 1, place_ref, ridge_ref, arrive, a_ref, l_ref, *scratch)


def chol_kernel(fly, sub, place_ref, ridge_ref, gram_ref, near_ref, out_ref, norm_ref, a_ref, l_ref, *rest):
    *scratch, tile_ref, sems = rest
    share, columns = out_ref.shape
    blocks = columns // BLK
    piece = a_ref.shape[0] // (fly * sub)
    stride = piece * fly
    starts = span_starts(blocks)
    spans = len(starts) - 1

    def start(i, _):
        s, f = i // fly, i % fly
        pltpu.make_async_copy(
            gram_ref.at[f * sub + s, pl.ds(0, piece)],
            a_ref.at[pl.ds(pl.multiple_of(i * piece, 8), piece)],
            sems.at[s],
        ).start()
        return 0

    known = near_ref.shape[1]
    near_copy = pltpu.make_async_copy(near_ref, l_ref.at[:, pl.ds(0, known)], sems.at[sub + 1])
    near_copy.start()
    lax.fori_loop(0, fly * sub, start, 0)
    norm_copy = pltpu.make_async_copy(gram_ref.at[:, pl.ds(piece, 8)], tile_ref, sems.at[sub])
    norm_copy.start()
    near_copy.wait()
    arrived = set()

    def arrive(q):
        end = sum(blocks - i for i in range(NEAR, starts[q + 1])) * BLK
        for s in range(min(pl.cdiv(end, stride), sub)):
            if s not in arrived:
                arrived.add(s)
                at = pl.ds(s * stride, stride)
                pltpu.make_async_copy(a_ref.at[at], a_ref.at[at], sems.at[s]).wait()

    panels(1, spans, place_ref, ridge_ref, arrive, a_ref, l_ref, *scratch)
    for s in range(sub):
        if s not in arrived:
            at = pl.ds(s * stride, stride)
            pltpu.make_async_copy(a_ref.at[at], a_ref.at[at], sems.at[s]).wait()
    norm_copy.wait()
    for g in range(norm_ref.shape[0]):
        members = range(g * BLK // share, (g + 1) * BLK // share)
        norm_ref[g : g + 1, :] = sum(tile_ref[i, 0:1, :] for i in members)
    mine = place_ref[0] * share
    at = pl.ds(pl.multiple_of(mine, share), share)
    row = lax.broadcasted_iota(jnp.int32, (share, BLK), 0) + mine
    col = lax.broadcasted_iota(jnp.int32, (share, BLK), 1)
    for c in range(0, columns, BLK):
        value = l_ref[at, 2 * c : 2 * c + BLK].astype(F32) + l_ref[at, 2 * c + BLK : 2 * c + 2 * BLK].astype(F32)
        out_ref[:, c : c + BLK] = jnp.where(col + c <= row, value, 0.0)


def chol_scratch(columns):
    return [
        pltpu.VMEM((columns, max(NEAR, SPAN) * BLK), F32),
        pltpu.VMEM((BLK, BLK), F32),
        pltpu.VMEM((BLK, BLK), F32),
        pltpu.VMEM((2, BLK, BLK), F32),
        pltpu.VMEM((272, BLK), F32),
        pltpu.VMEM((SPAN * BLK, SPAN * BLK), F32),
    ]


def factored_near(place, ridge, own, other, fly, sub, columns):
    smem, hbm = pl.BlockSpec(memory_space=pltpu.SMEM), pl.BlockSpec(memory_space=pl.ANY)
    rows = len(spread_rows(columns // BLK, 0, NEAR, sub)) * BLK
    return pl.pallas_call(
        functools.partial(near_kernel, fly, sub),
        out_shape=jax.ShapeDtypeStruct((columns, 2 * NEAR * BLK), BF16),
        in_specs=[smem, smem, hbm, hbm],
        scratch_shapes=[pltpu.VMEM((rows, BLK), F32)] + chol_scratch(columns) + [pltpu.SemaphoreType.DMA],
        compiler_params=pltpu.CompilerParams(vmem_limit_bytes=52 << 20),
        cost_estimate=pl.CostEstimate(flops=16 * 10**9, bytes_accessed=8 * 10**6, transcendentals=0),
        name="cholesky_first",
    )(place, ridge, own, other)


def factored(place, ridge, full, near, fly, sub, share):
    columns = share * fly * sub
    smem, hbm = pl.BlockSpec(memory_space=pltpu.SMEM), pl.BlockSpec(memory_space=pl.ANY)
    rows = len(spread_rows(columns // BLK, NEAR, columns // BLK, sub)) * BLK
    return pl.pallas_call(
        functools.partial(chol_kernel, fly, sub),
        out_shape=[
            jax.ShapeDtypeStruct((share, columns), F32),
            jax.ShapeDtypeStruct((columns // BLK, BLK), F32),
        ],
        in_specs=[smem, smem, hbm, hbm],
        scratch_shapes=[pltpu.VMEM((rows, BLK), F32), pltpu.VMEM((columns, 2 * columns), BF16)]
        + chol_scratch(columns)
        + [pltpu.VMEM((fly * sub, 8, BLK), F32), pltpu.SemaphoreType.DMA((sub + 2,))],
        compiler_params=pltpu.CompilerParams(vmem_limit_bytes=52 << 20),
        name="cholesky_rest",
    )(place, ridge, full, near)


def across_kernel(slot_ref, x_ref, table_ref, local_ref, out_ref, norm_ref, mixed_ref):
    devices = table_ref.shape[0]
    length = x_ref.shape[1]
    here = x_ref.shape[0] // devices
    per = here - 8
    picks = out_ref.shape[0] * BLK // (per * devices)
    join = BLK // picks
    lanes = lax.broadcasted_iota(jnp.int32, VREG, 1)
    norms = jnp.zeros(VREG, F32)
    total = devices * length
    table, local = table_ref[...], local_ref[...]
    groups = devices // join
    owner = lax.broadcasted_iota(jnp.int32, (groups, BLK), 1) // picks

    def chosen(parts):
        out = parts[0]
        for j in range(1, join):
            out = jnp.where(owner == j, parts[j], out)
        return out

    numbers = []
    for j in range(join):
        value = x_ref[pl.ds(per + here * j, groups, stride=here * join), :]
        numbers.append(pltpu.roll(value, picks * j, 1) if j else value)
    index = chosen(numbers).astype(jnp.int32)

    def product(a, b):
        return sum(contract(*pair, NN) for pair in zip(a, b))

    for col in range(per):
        rows = x_ref[pl.ds(col, devices, stride=here), :]
        squares = jnp.sum(jnp.sum(rows * rows, axis=0, keepdims=True), axis=1, keepdims=True)
        norm = jnp.sqrt(jnp.broadcast_to(squares, VREG) / total + 1e-06)
        norms = jnp.where(lanes == col, norm, norms)
        scale = 1.0 / (norm[0:1, :] * math.sqrt(total))
        mixed = product([table] * 3, thirds(rows))
        mixed_ref[...] = product(thirds(mixed), [local] * 3) * scale
        taken = [
            jnp.take_along_axis(
                mixed_ref[pl.ds(j, groups, stride=join), :], index, axis=1, mode="promise_in_bounds"
            )
            for j in range(join)
        ]
        out_ref[pl.ds(col, groups, stride=per), :] = chosen(taken)
    norm_ref[...] = pltpu.roll(norms, slot_ref[0], 1)


def across(slot, x, table, local, samples_all):
    devices = table.shape[0]
    per = x.shape[0] // devices - 8
    return pl.pallas_call(
        across_kernel,
        out_shape=[
            jax.ShapeDtypeStruct((samples_all * per // BLK, BLK), F32),
            jax.ShapeDtypeStruct(VREG, F32),
        ],
        in_specs=[pl.BlockSpec(memory_space=pltpu.SMEM)] + [pl.BlockSpec(memory_space=pltpu.VMEM)] * 3,
        scratch_shapes=[pltpu.VMEM((devices, BLK), F32)],
        compiler_params=pltpu.CompilerParams(vmem_limit_bytes=32 << 20),
        name="across_devices",
    )(slot, x, table, local)


def gram_kernel(fly, per, sizes, sub_ref, table_ref, *refs):
    parts, out_ref, high_ref, rest_ref = refs[:-3], refs[-3], refs[-2], refs[-1]
    sub = sub_ref[0]
    columns = high_ref.shape[0]
    blocks = columns // BLK
    depth = high_ref.shape[1] // BLK
    for i, ref in enumerate(parts):
        core = i // (len(parts) // 2)
        step = i % (len(parts) // 2) * 2
        source = (jnp.where(sub % 2 == 0, sub + core, sub - core) - step + len(parts)) % len(parts)
        for f in range(fly):
            at = pl.ds(pl.multiple_of((f * len(parts) + source) * per, per), per)
            for h in range(depth):
                row = (f * depth + h) * per
                high, rest = halves(ref[row : row + per, :])
                high_ref[at, h * BLK : (h + 1) * BLK] = high
                rest_ref[at, h * BLK : (h + 1) * BLK] = rest

    def block(index):
        at = pl.ds(pl.multiple_of(index * BLK, BLK), BLK)
        return high_ref[at, :], rest_ref[at, :]

    counts = [size * fly // BLK for size in sizes]
    start = 0
    for n, size in enumerate(sizes):
        for j in range(counts[n]):
            entry = 2 * (sub * sum(counts) + sum(counts[:n]) + j)
            value = contract_split(block(table_ref[entry]), block(table_ref[entry + 1]), NT)
            row = j * BLK
            while row < (j + 1) * BLK:
                f, inside = row // size, row % size
                many = min(size - inside, (j + 1) * BLK - row)
                at = f * sum(sizes) + start + inside
                out_ref[at : at + many, :] = value[row - j * BLK : row - j * BLK + many]
                row += many
        start += size


def gram_share(sub, parts, fly, per, lists):
    each = [len(found) // len(parts) for found in lists]
    table = [entry for s in range(len(parts)) for n, found in zip(each, lists) for entry in found[s * n : (s + 1) * n]]
    sizes = [n * BLK // fly for n in each]
    columns = fly * len(parts) * per
    depth = parts[0].shape[0] // (fly * per) * BLK
    return pl.pallas_call(
        functools.partial(gram_kernel, fly, per, sizes),
        out_shape=jax.ShapeDtypeStruct((sum(each) * BLK, BLK), F32),
        in_specs=[pl.BlockSpec(memory_space=pltpu.SMEM)] * 2
        + [pl.BlockSpec(memory_space=pltpu.VMEM)] * len(parts),
        scratch_shapes=[pltpu.VMEM((columns, depth), BF16)] * 2,
        compiler_params=pltpu.CompilerParams(vmem_limit_bytes=32 << 20),
        name="gram_share",
    )(sub, jnp.asarray(np.array(table, np.int32).reshape(-1)), *parts)


def shards(matrix, row_signs, sample_idx, ridge_shift):
    rows_here, columns = matrix.shape
    fly, sub = lax.axis_size("fly"), lax.axis_size("sub")
    devices = fly * sub
    place = lax.axis_index(AXES)
    samples = sample_idx.shape[0]
    samples_all = samples * devices
    per = columns // devices
    signed = (matrix * row_signs.astype(F32)[:, None]).T.reshape(devices, per, rows_here)
    numbers = jnp.zeros((8, rows_here), F32).at[0, :samples].set(sample_idx.astype(F32))
    numbers = jnp.broadcast_to(numbers[None], (devices, 8, rows_here))
    spread = lax.all_to_all(jnp.concatenate([signed, numbers], axis=1), AXES, 0, 0, tiled=True)
    table = jnp.asarray(sylvester(devices), BF16)
    local = jnp.asarray(sylvester(rows_here), BF16)
    slot = (place * per % BLK).astype(jnp.int32)[None]
    picked, norms = across(slot, spread.reshape(-1, rows_here), table, local, samples_all)
    mine = lax.all_to_all(picked.reshape(fly, -1, BLK), "fly", 0, 0, tiled=True).reshape(-1, BLK)
    parts = [mine]
    for step in range(2, sub, 2):
        parts.append(lax.ppermute(mine, "sub", [(i, (i + step) % sub) for i in range(sub)]))
    parts += [lax.ppermute(value, "sub", [(i, i ^ 1) for i in range(sub)]) for value in parts]
    blocks = columns // BLK
    lists = [spread_rows(blocks, 0, NEAR, sub), spread_rows(blocks, NEAR, blocks, sub)]
    share = gram_share(lax.axis_index("sub").astype(jnp.int32)[None], parts, fly, per, lists)
    pieces = lax.all_to_all(share.reshape(fly, -1, BLK), "fly", 0, 0, tiled=True)
    summed = jnp.sum(pieces, axis=0) / samples_all
    size = len(lists[0]) // sub * BLK // fly
    full = lax.all_gather(jnp.concatenate([summed[size:], norms], axis=0), AXES)
    near = [summed[:size]]
    for step in range(2, sub, 2):
        near.append(lax.ppermute(near[0], "sub", [(i, (i + step) % sub) for i in range(sub)]))
    near = jnp.broadcast_to(jnp.stack(near)[None], (fly, sub // 2, size, BLK))
    own = lax.all_to_all(near, "fly", 0, 0, tiled=True)
    other = lax.ppermute(own, "sub", [(i, i ^ 1) for i in range(sub)])
    index = place.astype(jnp.int32)[None]
    first = factored_near(index, ridge_shift, own, other, fly, sub, columns)
    chol, col_norms = factored(index, ridge_shift, full, first, fly, sub, per)
    return (chol, col_norms.reshape(columns))


def solution(mesh):
    in_specs = (P(AXES, None), P(AXES), P(AXES), P())
    out_specs = (P(AXES, None), P())
    return jax.shard_map(shards, mesh=mesh, in_specs=in_specs, out_specs=out_specs, check_vma=False)
```
